512 devices in a mesh: pipe: 16 (over z), dp: 32 (over x, y, core).
Axes of the slice: x: 4, y: 4, z: 16, core: 2. Of those that a mesh axis runs over, the one named last changes fastest.
Arguments:
- sent_base: bfloat16 [16, 256, 4096], P('pipe', None, 'dp'), may hold values from -13 to 13, as said below
- sent_part: bfloat16 [16, 256, 4096], P('pipe', None, 'dp'), may hold values from -4 to 4
- cot_base: bfloat16 [16, 256, 4096], P('pipe', None, 'dp'), may hold values from -7 to 7
- cot_part: bfloat16 [16, 256, 4096], P('pipe', None, 'dp'), may hold values from -7 to 7
- norm_gain: bfloat16 [16, 4096], P('pipe', 'dp'), may hold values from 0.25 to 1.75
- up_blocks: bfloat16 [16, 128, 64, 2048], P('pipe', 'dp'), may hold values from -2 to 2, as said below
- down_blocks: bfloat16 [16, 128, 64, 2048], P('pipe', 'dp'), may hold values from -2 to 2, as said below
- up_index: int32 [16, 128, 32], P('pipe', 'dp'), may hold values from 0 to 63, as said below
- down_index: int32 [16, 128, 32], P('pipe', 'dp'), may hold values from 0 to 63, as said below
Outputs:
- out_base: bfloat16 [16, 256, 4096], P('pipe', None, 'dp')
- out_part: bfloat16 [16, 256, 4096], P('pipe', None, 'dp')
- back_base: bfloat16 [16, 256, 4096], P('pipe', None, 'dp')
- back_part: bfloat16 [16, 256, 4096], P('pipe', None, 'dp')
- up_grad: bfloat16 [16, 128, 64, 2048], P('pipe', 'dp')
- down_grad: bfloat16 [16, 128, 64, 2048], P('pipe', 'dp')
- gain_gradient: float32 [16, 4096], P('pipe', 'dp')
The draws below stay inside these ranges and needn't reach their ends.
Inputs may be any that keep to these rules, and one draw needn't show every extreme that they name: `up_index`: each row of the last dimension lists 32 different block indices in increasing order, so that half of the blocks of each block column of the up projection are kept. `down_index`: each row of the last dimension lists 32 different block indices in increasing order, so that half of the blocks of each block row of the down projection are kept. `sent_base`: token rows of order one. `up_blocks`: entries of standard deviation one over the square root of 2048. `down_blocks`: entries of standard deviation one over the square root of 4096.
All inputs are finite; a program needn't handle non-finite values.
Results may differ from the reference program's by a relative error of at most 0.019.
Values may be sent and summed in bfloat16 or wider, within the bound.
No kernel may reach another device: no remote copies, remote signals or barrier semaphores. Data moves between devices by JAX's collectives and lax.ppermute only.
A program may use at most 128 MiB of HBM per device.

```python
import math
import jax
import jax.numpy as jnp
from jax import lax

D = 4096
BLK = 64
TOK = 256
HALF = 8192
NBLK = 64
KEPT = 32
HBLK = 128
N_PIPE = 16
N_DP = 32


tie_share = 0.9


row_share = 0.85


def kept_rows(key):
    split_keys = jax.random.split(key, N_PIPE * HBLK)
    orders = jax.vmap(lambda single: jax.random.permutation(single, NBLK))(split_keys)
    chosen = jnp.sort(orders[:, :KEPT], axis=-1)
    return chosen.reshape(N_PIPE, HBLK, KEPT).astype(jnp.int32)


def up_pattern(key):
    return kept_rows(jax.random.fold_in(key, 11))


def down_pattern(key):
    return kept_rows(jax.random.fold_in(key, 23))


def parent_section(key, section):
    stream = jax.random.fold_in(jax.random.fold_in(key, 41), section)
    return jnp.clip(jax.random.normal(stream, (HBLK, BLK, KEPT, BLK), jnp.float32), -6.0, 6.0)


def core_field(key):
    stream = jax.random.fold_in(key, 13)
    return jnp.clip(jax.random.normal(stream, (N_PIPE, TOK, D), jnp.float32), -5.0, 5.0)


def draw_up_index(key, part):
    return up_pattern(key)


def draw_down_index(key, part):
    return down_pattern(key)


def draw_up_blocks(key, part):
    spread_factor = (2.0 / D) ** 0.5

    def per_section(section):
        return parent_section(key, section) * spread_factor
    sections = jnp.arange(N_PIPE, dtype=jnp.int32)
    return lax.map(per_section, sections).reshape(N_PIPE, HBLK, BLK, KEPT * BLK).astype(jnp.bfloat16)


def draw_down_blocks(key, part):
    up_rows = up_pattern(key)
    down_rows = down_pattern(key)
    own_key = jax.random.fold_in(key, 29)
    matches = (down_rows[:, :, :, None] == up_rows[:, :, None, :]).astype(jnp.int32)
    shared = jnp.max(matches, axis=-1)
    position = jnp.argmax(matches, axis=-1).astype(jnp.int32)
    spread_factor = (2.0 / HALF) ** 0.5
    fresh_share = math.sqrt(1.0 - tie_share * tie_share)

    def per_section(section):
        parent = parent_section(key, section)
        picks = jnp.broadcast_to(position[section][:, None, :, None], (HBLK, BLK, KEPT, BLK))
        taken = jnp.take_along_axis(parent, picks, axis=2)
        fresh = jnp.clip(jax.random.normal(jax.random.fold_in(own_key, section), (HBLK, BLK, KEPT, BLK), jnp.float32), -6.0, 6.0)
        tied = jnp.where(shared[section][:, None, :, None] > 0, tie_share * taken + fresh_share * fresh, fresh)
        return jnp.clip(tied, -6.0, 6.0) * spread_factor
    sections = jnp.arange(N_PIPE, dtype=jnp.int32)
    return lax.map(per_section, sections).reshape(N_PIPE, HBLK, BLK, KEPT * BLK).astype(jnp.bfloat16)


def draw_sent_base(key, part):
    core_rows = core_field(key)
    return core_rows.astype(jnp.bfloat16)


def leaning_cotangent(key, noise_part):
    leading = jnp.roll(core_field(key), 1, axis=0)
    return row_share * leading + math.sqrt(1.0 - row_share * row_share) * noise_part


def draw_cot_base(key, part):
    own_key = jax.random.fold_in(key, 37)
    noise_part = jnp.clip(jax.random.normal(own_key, (N_PIPE, TOK, D), jnp.float32), -5.0, 5.0)
    return leaning_cotangent(key, noise_part).astype(jnp.bfloat16)


def draw_cot_part(key, part):
    own_key = jax.random.fold_in(key, 43)
    noise_part = jnp.clip(jax.random.normal(own_key, (N_PIPE, TOK, D), jnp.float32), -5.0, 5.0)
    return leaning_cotangent(key, noise_part).astype(jnp.bfloat16)


def shard_levels(key, shape, cuts, least, high):
    factor_of, own = 1.0, jax.random.fold_in(key, 6)
    for dim, parts in cuts:
        steps = jnp.exp(jax.random.uniform(jax.random.fold_in(own, dim), (parts,), jnp.float32, least / len(cuts), high / len(cuts)))
        factor_of = factor_of * jnp.repeat(steps, shape[dim] // parts).reshape([-1 if axis == dim else 1 for axis in range(len(shape))])
    return factor_of


def noise(key, dims, scale, most, cuts=(), kind=jnp.bfloat16):
    values = scale * jax.random.normal(key, dims, jnp.float32)
    if cuts:
        values = values * shard_levels(key, dims, cuts, -0.22, 0.18)
    return jnp.clip(values, -most, most).astype(kind)


def setup_inputs(seed: int = 0) -> dict:
    splits = jax.random.split(jax.random.key(seed), 10)
    sent_base = draw_sent_base(jax.random.fold_in(splits[9], 71), 0)
    sent_part = noise(splits[1], (N_PIPE, TOK, D), 0.5, 4.0, ((0, 16), (2, 32)))
    cot_base = draw_cot_base(jax.random.fold_in(splits[9], 71), 0)
    cot_part = draw_cot_part(jax.random.fold_in(splits[9], 71), 0)
    norm_gain = jnp.clip(1.0 + 0.15 * jax.random.normal(splits[4], (N_PIPE, D), jnp.float32), 0.25, 1.75).astype(jnp.bfloat16)
    up_blocks = draw_up_blocks(jax.random.fold_in(splits[9], 71), 0)
    down_blocks = draw_down_blocks(jax.random.fold_in(splits[9], 71), 0)
    up_index = draw_up_index(jax.random.fold_in(splits[9], 71), 0)
    down_index = draw_down_index(jax.random.fold_in(splits[9], 71), 0)
    return {"sent_base": sent_base, "sent_part": sent_part, "cot_base": cot_base, "cot_part": cot_part, "norm_gain": norm_gain, "up_blocks": up_blocks, "down_blocks": down_blocks, "up_index": up_index, "down_index": down_index}


eps = 1e-05

def place_groups(values, index, groups, nblk):
    tokens = values.shape[0]
    blk = values.shape[2] // index.shape[1]
    per = index.shape[0] * index.shape[1] // groups
    pieces = values.reshape(tokens, groups, per, blk)
    onehot = (index.reshape(groups, per)[:, :, None] == jnp.arange(nblk)[None, None, :]).astype(jnp.float32)
    spread = jnp.einsum('tjmo,jmb->jtbo', pieces, onehot, precision=lax.Precision.HIGHEST)
    rounded = spread.astype(jnp.bfloat16).astype(jnp.float32)
    return lax.optimization_barrier(jnp.sum(rounded, axis=0)).reshape(tokens, nblk * blk)

def one_section(operands):
    section, base, part, gain, w_up, w_down, idx_up, idx_down, g_out_base, g_out_part = operands
    odd = (section % 2).astype(jnp.float32)
    tokens, width = base.shape
    hblk, blk, _ = w_up.shape
    kept = idx_up.shape[1]
    nblk = width // blk
    complete_input = base.astype(jnp.float32)
    root_mean_square = jnp.sqrt(lax.optimization_barrier(jnp.mean(complete_input * complete_input, axis=-1, keepdims=True)) + eps)
    scaled_input = complete_input / root_mean_square
    gain_wide = gain.astype(jnp.float32)
    normalized_rows = (scaled_input * gain_wide).astype(jnp.bfloat16)
    gathered = normalized_rows.reshape(tokens, nblk, blk)[:, idx_up].reshape(tokens, hblk, kept * blk)
    pre = jnp.einsum('tcm,com->tco', gathered.astype(jnp.float32), w_up.astype(jnp.float32))
    hidden = jax.nn.silu(pre).astype(jnp.bfloat16)
    terms = jnp.einsum('tci,cim->tcm', hidden.astype(jnp.float32), w_down.astype(jnp.float32))
    ffn = place_groups(terms, idx_down, N_DP, nblk)
    out_base = (complete_input + odd * (part.astype(jnp.float32) + ffn)).astype(jnp.bfloat16)
    out_part = ((1.0 - odd) * ffn).astype(jnp.bfloat16)
    column_block = g_out_base.astype(jnp.float32)
    g_ffn = (odd * column_block + (1.0 - odd) * g_out_part.astype(jnp.float32)).astype(jnp.bfloat16)
    g_gathered = g_ffn.reshape(tokens, nblk, blk)[:, idx_down].reshape(tokens, hblk, kept * blk)
    down_grad = jnp.einsum('tci,tcm->cim', hidden.astype(jnp.float32), g_gathered.astype(jnp.float32)).astype(jnp.bfloat16)
    g_hidden = jnp.einsum('tcm,cim->tci', g_gathered.astype(jnp.float32), w_down.astype(jnp.float32))
    sig = jax.nn.sigmoid(pre)
    g_pre = (g_hidden * sig * (1.0 + pre * (1.0 - sig))).astype(jnp.bfloat16)
    up_grad = jnp.einsum('tco,tcm->com', g_pre.astype(jnp.float32), gathered.astype(jnp.float32)).astype(jnp.bfloat16)
    back_terms = jnp.einsum('tco,com->tcm', g_pre.astype(jnp.float32), w_up.astype(jnp.float32))
    normalized_gradient = place_groups(back_terms, idx_up, N_DP, nblk)
    centered_gradient = normalized_gradient * gain_wide
    row_statistic = lax.optimization_barrier(jnp.mean(centered_gradient * scaled_input, axis=-1, keepdims=True))
    base_gradient = ((centered_gradient - scaled_input * row_statistic) / root_mean_square + column_block).astype(jnp.bfloat16)
    g_part = (odd * column_block).astype(jnp.bfloat16)
    gain_gradient = lax.optimization_barrier(jnp.sum(normalized_gradient * scaled_input, axis=0))
    return (out_base, out_part, base_gradient, g_part, up_grad, down_grad, gain_gradient)

def reference(sent_base, sent_part, cot_base, cot_part, norm_gain, up_blocks, down_blocks, up_index, down_index):
    base = jnp.roll(sent_base, 1, axis=0)
    part = jnp.roll(sent_part, 1, axis=0)
    sections = jnp.arange(sent_base.shape[0], dtype=jnp.int32)
    results = lax.map(one_section, (sections, base, part, norm_gain, up_blocks, down_blocks, up_index, down_index, cot_base, cot_part))
    out_base, out_part, base_gradient, g_part, up_grad, down_grad, gain_gradient = results
    back_base = jnp.roll(base_gradient, -1, axis=0)
    back_part = jnp.roll(g_part, -1, axis=0)
    return (out_base, out_part, back_base, back_part, up_grad, down_grad, gain_gradient)
```

```python
import functools

import jax
import jax.numpy as jnp
from jax import lax
from jax.experimental import pallas as pl
from jax.experimental.pallas import tpu as pltpu
from jax.sharding import PartitionSpec as P

eps = 1e-05
LANES = 128
EXTRA = 16
F32 = jnp.float32
BF16 = jnp.bfloat16
VMEM = pl.BlockSpec(memory_space=pltpu.VMEM)
SMEM = pl.BlockSpec(memory_space=pltpu.SMEM)
HBM = pl.BlockSpec(memory_space=pltpu.HBM)
PARAMS = pltpu.CompilerParams(vmem_limit_bytes=40 * 1024 * 1024)


def passed_along(shard, axis, by):
    count = lax.axis_size(axis)
    return lax.ppermute(shard, axis, [(i, (i + by) % count) for i in range(count)])


def other_core(shard):
    count = lax.axis_size("dp")
    return lax.ppermute(shard, "dp", [(i, i ^ 1) for i in range(count)])


def after(value, earlier):
    return lax.optimization_barrier((value, earlier))[0]


def exchange(chunks):
    return lax.all_to_all(chunks, "dp", 0, 0, tiled=True)


def pack_kernel(odd_ref, base_ref, cot_base_ref, cot_part_ref, gain_ref, out_ref):
    count, rows, _ = out_ref.shape
    half = base_ref.shape[0] // 2
    odd = odd_ref[0] == 1
    gain = jnp.broadcast_to(gain_ref[...].astype(F32), (EXTRA, LANES)).astype(BF16)
    for j in range(count):
        at = pl.ds((j % 2) * half, half)
        out_ref[j, :half, :] = base_ref[at, :]
        out_ref[j, half : 2 * half, :] = jnp.where(odd, cot_base_ref[at, :], cot_part_ref[at, :])
        out_ref[j, 2 * half :, :] = gain


def pack(odd, base, cot_base, cot_part, gain, count):
    return pl.pallas_call(
        pack_kernel,
        out_shape=jax.ShapeDtypeStruct((count, base.shape[0] + EXTRA, LANES), BF16),
        in_specs=[SMEM, VMEM, VMEM, VMEM, VMEM],
        out_specs=VMEM,
        compiler_params=PARAMS,
        cost_estimate=pl.CostEstimate(flops=1_000_000, bytes_accessed=2_500_000, transcendentals=0),
        name="pack_chunks",
    )(odd[None], base, cot_base, cot_part, gain)


def merge_tiles(tile0, tile1, turned0, turned1, kept0, kept1, lower):
    low = jnp.where(lower, 1.0, 0.0).astype(BF16)
    high = jnp.where(lower, 0.0, 1.0).astype(BF16)
    swapped = tile1 * low + tile0 * high
    swapped = jnp.concatenate([swapped[:, 64:], swapped[:, :64]], axis=1)
    first = jnp.where(lower, kept0 * (1 - turned0), 0).astype(F32).astype(BF16)
    second = jnp.where(lower, 0, kept1 * (1 - turned1)).astype(F32).astype(BF16)
    third = jnp.where(lower, kept0 * turned0, kept1 * turned1).astype(F32).astype(BF16)
    return tile0 * first + tile1 * second + swapped * third


def tile_at(n):
    return pl.ds(pl.multiple_of(n * LANES, LANES), LANES)


def densify_kernel(idx_up, idx_down, up_ref, down_ref, out_ref, dense, sems):
    hblk, blk, wide = up_ref.shape
    kept = idx_up.shape[1]
    tiles = out_ref.shape[1] // LANES
    units = hblk * blk
    lower = lax.broadcasted_iota(jnp.int32, (1, LANES), 1) < blk
    copies = []
    for which, (idx, src) in enumerate(((idx_up, up_ref), (idx_down, down_ref))):

        def step(j, ats, which=which, idx=idx, src=src):
            plans, next_ats = [], []
            for c in range(hblk):
                p0 = jnp.minimum(ats[c], kept - 1)
                m0 = jnp.where((ats[c] < kept) & (idx[c, p0] == 2 * j), 1, 0)
                middle = ats[c] + m0
                p1 = jnp.minimum(middle, kept - 1)
                m1 = jnp.where((middle < kept) & (idx[c, p1] == 2 * j + 1), 1, 0)
                plans.append((p0, m0, p1, m1))
                next_ats.append(middle + m1)
            loaded = [
                (src[c, :, tile_at(p0 // 2)], src[c, :, tile_at(p1 // 2)])
                for c, (p0, m0, p1, m1) in enumerate(plans)
            ]
            merged = [
                merge_tiles(tile0, tile1, p0 % 2, 1 - p1 % 2, m0, m1, lower)
                for (tile0, tile1), (p0, m0, p1, m1) in zip(loaded, plans)
            ]
            for c in range(hblk):
                dense[pl.ds(which * units + c * blk, blk), tile_at(j)] = merged[c]
            return tuple(next_ats)

        lax.fori_loop(0, tiles, step, (jnp.int32(0),) * hblk, unroll=2)
        rows = pl.ds(which * units, units)
        copies.append(pltpu.make_async_copy(dense.at[rows], out_ref.at[rows], sems.at[which]))
        copies[-1].start()
    for copy in copies:
        copy.wait()


def densify(idx_up, idx_down, up, down, width):
    hblk, blk, _ = up.shape
    return pl.pallas_call(
        densify_kernel,
        out_shape=jax.ShapeDtypeStruct((2 * hblk * blk, width), BF16),
        in_specs=[SMEM, SMEM, VMEM, VMEM],
        out_specs=HBM,
        scratch_shapes=[pltpu.VMEM((2 * hblk * blk, width), BF16), pltpu.SemaphoreType.DMA((2,))],
        compiler_params=PARAMS,
        cost_estimate=pl.CostEstimate(flops=10_000_000, bytes_accessed=6_291_456, transcendentals=0),
        name="densify",
    )(idx_up, idx_down, up, down)


def dot_nt(a, b):
    return lax.dot_general(a, b, (((1,), (1,)), ((), ())), preferred_element_type=F32)


def dot_nn(a, b):
    return lax.dot_general(a, b, (((1,), (0,)), ((), ())), preferred_element_type=F32)


def split3(value):
    high = value.astype(BF16).astype(F32)
    rest = value - high
    middle = rest.astype(BF16).astype(F32)
    return high, middle, rest - middle


def main_kernel(
    rows_ref, own_hbm, other_hbm, back_hbm, swap_ref, keep_ref, weights, back_ref, in_sems, out_sems
):
    count = rows_ref.shape[0]
    tokens = (rows_ref.shape[1] - EXTRA) // 2
    width = count * LANES
    units = own_hbm.shape[0] // 2
    loads = []
    for n, (source, which) in enumerate(((own_hbm, 0), (other_hbm, 0), (own_hbm, 1), (other_hbm, 1))):
        loads.append(
            pltpu.make_async_copy(
                source.at[pl.ds(which * units, units)], weights.at[n], in_sems.at[n]
            )
        )
        loads[-1].start()
    squares = jnp.zeros((tokens, LANES), F32)
    for j in range(count):
        x = rows_ref[j, :tokens, :].astype(F32)
        squares = squares + x * x
    mean_square = jnp.sum(squares, axis=-1, keepdims=True) / width
    inverse = 1.0 / jnp.sqrt(mean_square + eps)
    for j in range(count):
        x = rows_ref[j, :tokens, :].astype(F32)
        gain = rows_ref[j, 2 * tokens :, :].astype(F32)[:1]
        swap_ref[j] = (x * inverse * gain).astype(BF16)
        swap_ref[count + j] = rows_ref[j, tokens : 2 * tokens, :]
    normed = jnp.concatenate([swap_ref[j] for j in range(count)], axis=1)
    g_rows = jnp.concatenate(
        [rows_ref[j, tokens : 2 * tokens, :] for j in range(count)], axis=1
    )
    pres, g_hiddens = [], []
    for n in range(2):
        loads[n].wait()
        pres.append(dot_nt(normed, weights[n]))
    for n in range(2):
        loads[2 + n].wait()
        g_hiddens.append(dot_nt(g_rows, weights[2 + n]))
    per = units // LANES
    stat = jnp.zeros((tokens, 1), F32)
    hiddens, g_pres = [], []
    for n, (pre, g_hidden) in enumerate(zip(pres, g_hiddens)):
        sig = 1.0 / (1.0 + jnp.exp(-pre))
        hidden = (pre * sig).astype(BF16)
        g_pre = (g_hidden * sig * (1.0 + pre * (1.0 - sig))).astype(BF16)
        stat = stat + jnp.sum(g_pre.astype(F32) * pre, axis=-1, keepdims=True)
        for k in range(per):
            at = slice(k * LANES, (k + 1) * LANES)
            if n == 0:
                keep_ref[k] = hidden[:, at]
                keep_ref[per + k] = g_pre[:, at]
            else:
                swap_ref[2 * count + k] = hidden[:, at]
                swap_ref[2 * count + per + k] = g_pre[:, at]
        hiddens.append(hidden)
        g_pres.append(g_pre)
    stat_high, stat_low, _ = split3(stat)
    lane = lax.broadcasted_iota(jnp.int32, (tokens, LANES), 1)
    columns = jnp.zeros((tokens, LANES), F32)
    for k, part in enumerate((stat_high, stat_low) + split3(inverse)):
        columns = jnp.where(lane == k, part, columns)
    riding = jnp.transpose(columns)[:EXTRA].astype(BF16)
    step = 1024
    stores = []
    for n, s in enumerate(range(0, width, step)):
        back = dot_nn(g_pres[0], weights[0, :, s : s + step]) + dot_nn(
            g_pres[1], weights[1, :, s : s + step]
        )
        ffn = dot_nn(hiddens[0], weights[2, :, s : s + step]) + dot_nn(
            hiddens[1], weights[3, :, s : s + step]
        )
        for k in range(step // LANES):
            j = s // LANES + k
            at = slice(k * LANES, (k + 1) * LANES)
            back_ref[j, :tokens, :] = back[:, at].astype(BF16)
            back_ref[j, tokens : 2 * tokens, :] = ffn[:, at].astype(BF16)
            back_ref[j, 2 * tokens :, :] = riding
        at = pl.ds(s // LANES, step // LANES)
        stores.append(pltpu.make_async_copy(back_ref.at[at], back_hbm.at[at], out_sems.at[n]))
        stores[-1].start()
    for store in stores:
        store.wait()


def main(rows, own, other):
    count = rows.shape[0]
    tokens = (rows.shape[1] - EXTRA) // 2
    units, width = own.shape[0] // 2, own.shape[1]
    per = units // LANES
    return pl.pallas_call(
        main_kernel,
        out_shape=(
            jax.ShapeDtypeStruct(rows.shape, BF16),
            jax.ShapeDtypeStruct((2 * count + 2 * per, tokens, LANES), BF16),
            jax.ShapeDtypeStruct((2 * per, tokens, LANES), BF16),
        ),
        in_specs=[VMEM, HBM, HBM],
        out_specs=[HBM, VMEM, VMEM],
        scratch_shapes=[
            pltpu.VMEM((4, units, width), BF16),
            pltpu.VMEM(rows.shape, BF16),
            pltpu.SemaphoreType.DMA((4,)),
            pltpu.SemaphoreType.DMA((width // 1024,)),
        ],
        compiler_params=PARAMS,
        cost_estimate=pl.CostEstimate(flops=2_200_000_000, bytes_accessed=16_000_000, transcendentals=65_536),
        name="forward_backward",
    )(rows, own, other)


def grads_kernel(idx_up, idx_down, mine_ref, keep_ref, theirs_ref, up_ref, down_ref, dense):
    hblk, blk, wide = up_ref.shape
    per = hblk * blk // LANES
    count = (mine_ref.shape[0] - 2 * per) // 2
    lower = lax.broadcasted_iota(jnp.int32, (1, LANES), 1) < blk
    group = 8

    def left(n):
        tiles = [
            jnp.concatenate([keep_ref[n * per + k], theirs_ref[2 * count + n * per + k]], axis=0)
            for k in range(per)
        ]
        return jnp.concatenate(tiles, axis=1)

    for n, first, idx, out in ((0, count, idx_down, down_ref), (1, 0, idx_up, up_ref)):
        turned = jnp.transpose(left(n))
        for s in range(0, count, group):
            rows = jnp.concatenate(
                [
                    jnp.concatenate([mine_ref[first + j], theirs_ref[first + j]], axis=0)
                    for j in range(s, s + group)
                ],
                axis=1,
            )
            dense[:, s * LANES : (s + group) * LANES] = dot_nn(turned, rows).astype(BF16)
        def step(j, carry, idx=idx, out=out):
            merged = []
            for c in range(hblk):
                e0, e1 = idx[c, 2 * j], idx[c, 2 * j + 1]
                rows = pl.ds(c * blk, blk)
                merged.append(
                    merge_tiles(
                        dense[rows, tile_at(e0 // 2)],
                        dense[rows, tile_at(e1 // 2)],
                        e0 % 2,
                        1 - e1 % 2,
                        1,
                        1,
                        lower,
                    )
                )
            for c in range(hblk):
                out[c, :, tile_at(j)] = merged[c]
            return carry

        lax.fori_loop(0, wide // LANES, step, 0, unroll=2)


def grads(idx_up, idx_down, mine, keep, theirs, shape, width):
    hblk, blk, _ = shape
    return pl.pallas_call(
        grads_kernel,
        out_shape=(jax.ShapeDtypeStruct(shape, BF16), jax.ShapeDtypeStruct(shape, BF16)),
        in_specs=[SMEM, SMEM, VMEM, VMEM, VMEM],
        out_specs=[VMEM, VMEM],
        scratch_shapes=[pltpu.VMEM((hblk * blk, width), BF16)],
        compiler_params=PARAMS,
        cost_estimate=pl.CostEstimate(flops=1_000_000, bytes_accessed=100_000, transcendentals=0),
        name="weight_gradients",
    )(idx_up, idx_down, mine, keep, theirs)


def finish_kernel(width, parts_ref, base_ref, gain_ref, cot_ref, out_ref, gain_out_ref):
    count = parts_ref.shape[0]
    tokens = (parts_ref.shape[1] - EXTRA) // 2
    gain = gain_ref[...].astype(F32)
    total_gain = jnp.zeros((1, LANES), F32)
    for half in range(2):
        total = jnp.zeros((tokens, LANES), F32)
        riding = jnp.zeros((EXTRA, LANES), F32)
        for j in range(half, count, 2):
            total = total + parts_ref[j, :tokens, :].astype(F32)
            riding = riding + parts_ref[j, 2 * tokens :, :].astype(F32)
        first = parts_ref[half, 2 * tokens :, :].astype(F32)
        summed = (riding[0:1] + riding[1:2]) / width
        inverse = first[2:3] + first[3:4] + first[4:5]
        row = lax.broadcasted_iota(jnp.int32, (LANES, LANES), 0)
        turned = jnp.transpose(jnp.where(row == 0, summed, jnp.where(row == 1, inverse, 0.0)))
        stat = turned[:, 0:1]
        inverse = turned[:, 1:2]
        at = pl.ds(half * tokens, tokens)
        scaled = base_ref[at, :].astype(F32) * inverse
        out_ref[at, :] = (
            (total * gain - scaled * stat) * inverse + cot_ref[at, :].astype(F32)
        ).astype(BF16)
        total_gain = total_gain + jnp.sum(total * scaled, axis=0, keepdims=True)
    gain_out_ref[...] = total_gain


def finish(parts, base, gain, cot, width):
    return pl.pallas_call(
        functools.partial(finish_kernel, width),
        out_shape=(
            jax.ShapeDtypeStruct(base.shape, BF16),
            jax.ShapeDtypeStruct((1, LANES), F32),
        ),
        in_specs=[VMEM] * 4,
        out_specs=[VMEM] * 2,
        compiler_params=PARAMS,
        cost_estimate=pl.CostEstimate(flops=2_000_000, bytes_accessed=1_500_000, transcendentals=0),
        name="input_gradient",
    )(parts, base, gain, cot)


def outputs_kernel(odd_ref, parts_ref, base_ref, part_ref, out_base_ref, out_part_ref):
    count = parts_ref.shape[0]
    tokens = (parts_ref.shape[1] - EXTRA) // 2
    odd = odd_ref[0].astype(F32)
    for half in range(2):
        total = jnp.zeros((tokens, LANES), F32)
        for j in range(half, count, 2):
            total = total + parts_ref[j, tokens : 2 * tokens, :].astype(F32)
        at = pl.ds(half * tokens, tokens)
        part = part_ref[at, :].astype(F32)
        out_base_ref[at, :] = (base_ref[at, :].astype(F32) + odd * (part + total)).astype(BF16)
        out_part_ref[at, :] = ((1.0 - odd) * total).astype(BF16)


def outputs(odd, parts, base, part):
    return pl.pallas_call(
        outputs_kernel,
        out_shape=(jax.ShapeDtypeStruct(base.shape, BF16), jax.ShapeDtypeStruct(base.shape, BF16)),
        in_specs=[SMEM, VMEM, VMEM, VMEM],
        out_specs=[VMEM] * 2,
        compiler_params=PARAMS,
        cost_estimate=pl.CostEstimate(flops=2_000_000, bytes_accessed=1_500_000, transcendentals=0),
        name="section_outputs",
    )(odd[None], parts, base, part)


def per_device(
    sent_base,
    sent_part,
    cot_base,
    cot_part,
    norm_gain,
    up_blocks,
    down_blocks,
    up_index,
    down_index,
):
    count = lax.axis_size("dp")
    tokens, lanes = sent_base.shape[1:]
    width = count * lanes
    odd = lax.axis_index("pipe") % 2

    arrived_base = passed_along(sent_base[0], "pipe", 1)
    own = densify(up_index[0], down_index[0], up_blocks[0], down_blocks[0], width)
    packed = pack(odd, after(arrived_base, own), cot_base[0], cot_part[0], norm_gain, count)
    rows = exchange(packed)
    other = other_core(after(own, packed))
    g_part = jnp.where(odd == 1, cot_base[0], jnp.zeros_like(cot_base[0]))
    back_part = passed_along(after(g_part, packed), "pipe", -1)
    arrived_part = passed_along(after(sent_part[0], packed), "pipe", 1)
    own_later, back_part, arrived_part = lax.optimization_barrier((own, back_part, arrived_part))

    parts, swap, keep = main(rows, own_later, other)
    theirs = other_core(swap)
    up_grad, down_grad = grads(
        up_index[0], down_index[0], swap, keep, theirs, up_blocks.shape[1:], width
    )
    part_rows = exchange(parts)
    up_grad, down_grad, part_rows = lax.optimization_barrier((up_grad, down_grad, part_rows))
    base_gradient, gain_gradient = finish(part_rows, arrived_base, norm_gain, cot_base[0], width)
    back_base = passed_along(base_gradient, "pipe", -1)
    out_base, out_part = outputs(odd, part_rows, arrived_base, arrived_part)
    return (
        out_base[None],
        out_part[None],
        back_base[None],
        back_part[None],
        up_grad[None],
        down_grad[None],
        gain_gradient,
    )


def solution(mesh):
    in_specs = (
        P("pipe", None, "dp"),
        P("pipe", None, "dp"),
        P("pipe", None, "dp"),
        P("pipe", None, "dp"),
        P("pipe", "dp"),
        P("pipe", "dp", None, None),
        P("pipe", "dp", None, None),
        P("pipe", "dp", None),
        P("pipe", "dp", None),
    )
    out_specs = (
        P("pipe", None, "dp"),
        P("pipe", None, "dp"),
        P("pipe", None, "dp"),
        P("pipe", None, "dp"),
        P("pipe", "dp", None, None),
        P("pipe", "dp", None, None),
        P("pipe", "dp"),
    )
    return jax.shard_map(
        per_device, mesh=mesh, in_specs=in_specs, out_specs=out_specs, check_vma=False
    )
```

```python
import functools

import jax
import jax.numpy as jnp
from jax import lax
from jax.experimental import pallas as pl
from jax.experimental.pallas import tpu as pltpu
from jax.sharding import PartitionSpec as P

eps = 1e-05
LANES = 128
MAIN_VMEM = 24
EXTRA = 16
F32 = jnp.float32
BF16 = jnp.bfloat16
VMEM = pl.BlockSpec(memory_space=pltpu.VMEM)
SMEM = pl.BlockSpec(memory_space=pltpu.SMEM)
HBM = pl.BlockSpec(memory_space=pltpu.HBM)
PARAMS = pltpu.CompilerParams(vmem_limit_bytes=40 * 1024 * 1024)


def passed_along(shard, axis, by):
    count = lax.axis_size(axis)
    return lax.ppermute(shard, axis, [(i, (i + by) % count) for i in range(count)])


def other_core(shard):
    count = lax.axis_size("dp")
    return lax.ppermute(shard, "dp", [(i, i ^ 1) for i in range(count)])


def after(value, earlier):
    return lax.optimization_barrier((value, earlier))[0]


def exchange(chunks):
    return lax.all_to_all(chunks, "dp", 0, 0, tiled=True)


def pack_kernel(odd_ref, cot_base_hbm, cot_part_hbm, gain_hbm, out_ref, cot_base_ref, cot_part_ref, gain_ref, chunk, sems, in_sems):
    count = out_ref.shape[0]
    loads = [
        pltpu.make_async_copy(source, target, in_sems.at[n])
        for n, (source, target) in enumerate(
            ((cot_base_hbm, cot_base_ref), (cot_part_hbm, cot_part_ref), (gain_hbm, gain_ref))
        )
    ]
    for load in loads:
        load.start()
    for load in loads:
        load.wait()
    half = cot_base_ref.shape[0] // 2
    odd = odd_ref[0] == 1
    copies = []
    for n in range(2):
        at = pl.ds(n * half, half)
        chunk[n, :half, :] = jnp.where(odd, cot_base_ref[at, :], cot_part_ref[at, :])
        chunk[n, half:, :] = jnp.broadcast_to(gain_ref[...].astype(F32), (EXTRA, LANES)).astype(BF16)
    for j in range(count):
        copies.append(
            pltpu.make_async_copy(
                chunk.at[j % 2], out_ref.at[j, pl.ds(half, half + EXTRA)], sems.at[j]
            )
        )
        copies[-1].start()
    for copy in copies:
        copy.wait()


def pack(odd, cot_base, cot_part, gain, count):
    tokens = cot_base.shape[0]
    return pl.pallas_call(
        pack_kernel,
        out_shape=jax.ShapeDtypeStruct((count, tokens + EXTRA, LANES), BF16),
        in_specs=[SMEM, HBM, HBM, HBM],
        out_specs=HBM,
        scratch_shapes=[
            pltpu.VMEM(cot_base.shape, BF16),
            pltpu.VMEM(cot_part.shape, BF16),
            pltpu.VMEM(gain.shape, BF16),
            pltpu.VMEM((2, tokens // 2 + EXTRA, LANES), BF16),
            pltpu.SemaphoreType.DMA((count,)),
            pltpu.SemaphoreType.DMA((3,)),
        ],
        compiler_params=pltpu.CompilerParams(vmem_limit_bytes=60 * 1024 * 1024),
        cost_estimate=pl.CostEstimate(flops=1_000_000, bytes_accessed=1_500_000, transcendentals=0),
        name="pack_cotangent",
    )(odd[None], cot_base, cot_part, gain)


def pack_base_kernel(base_ref, packed_ref, out_ref, sems):
    count = out_ref.shape[0]
    half = base_ref.shape[0] // 2
    copies = []
    for j in range(count):
        copies.append(
            pltpu.make_async_copy(
                base_ref.at[pl.ds((j % 2) * half, half)], out_ref.at[j, pl.ds(0, half)], sems.at[j]
            )
        )
        copies[-1].start()
    for copy in copies:
        copy.wait()


def pack_base(base, packed):
    count = packed.shape[0]
    return pl.pallas_call(
        pack_base_kernel,
        out_shape=jax.ShapeDtypeStruct(packed.shape, BF16),
        in_specs=[VMEM, HBM],
        out_specs=HBM,
        scratch_shapes=[pltpu.SemaphoreType.DMA((count,))],
        input_output_aliases={1: 0},
        compiler_params=pltpu.CompilerParams(vmem_limit_bytes=16 * 1024 * 1024),
        cost_estimate=pl.CostEstimate(flops=1_000, bytes_accessed=1_000_000, transcendentals=0),
        name="pack_base",
    )(base, packed)


def merge_tiles(tile0, tile1, turned0, turned1, kept0, kept1, lower):
    low = jnp.where(lower, 1.0, 0.0).astype(BF16)
    high = jnp.where(lower, 0.0, 1.0).astype(BF16)
    swapped = tile1 * low + tile0 * high
    swapped = jnp.concatenate([swapped[:, 64:], swapped[:, :64]], axis=1)
    first = jnp.where(lower, kept0 * (1 - turned0), 0).astype(F32).astype(BF16)
    second = jnp.where(lower, 0, kept1 * (1 - turned1)).astype(F32).astype(BF16)
    third = jnp.where(lower, kept0 * turned0, kept1 * turned1).astype(F32).astype(BF16)
    return tile0 * first + tile1 * second + swapped * third


def tile_at(n):
    return pl.ds(pl.multiple_of(n * LANES, LANES), LANES)


def densify_kernel(idx_up, idx_down, up_ref, down_ref, after_ref, dense_up, dense_down):
    hblk, blk, wide = up_ref.shape
    kept = idx_up.shape[1]
    tiles = dense_up.shape[1] // LANES
    lower = lax.broadcasted_iota(jnp.int32, (1, LANES), 1) < blk
    for idx, src, dense in ((idx_up, up_ref, dense_up), (idx_down, down_ref, dense_down)):

        def step(j, ats, idx=idx, src=src, dense=dense):
            plans, next_ats = [], []
            for c in range(hblk):
                p0 = jnp.minimum(ats[c], kept - 1)
                m0 = jnp.where((ats[c] < kept) & (idx[c, p0] == 2 * j), 1, 0)
                middle = ats[c] + m0
                p1 = jnp.minimum(middle, kept - 1)
                m1 = jnp.where((middle < kept) & (idx[c, p1] == 2 * j + 1), 1, 0)
                plans.append((p0, m0, p1, m1))
                next_ats.append(middle + m1)
            loaded = [
                (src[c, :, tile_at(p0 // 2)], src[c, :, tile_at(p1 // 2)])
                for c, (p0, m0, p1, m1) in enumerate(plans)
            ]
            merged = [
                merge_tiles(tile0, tile1, p0 % 2, 1 - p1 % 2, m0, m1, lower)
                for (tile0, tile1), (p0, m0, p1, m1) in zip(loaded, plans)
            ]
            for c in range(hblk):
                dense[pl.ds(c * blk, blk), tile_at(j)] = merged[c]
            return tuple(next_ats)

        lax.fori_loop(0, tiles, step, (jnp.int32(0),) * hblk, unroll=2)


def densify(idx_up, idx_down, up, down, width, earlier):
    hblk, blk, _ = up.shape
    return pl.pallas_call(
        densify_kernel,
        out_shape=[jax.ShapeDtypeStruct((hblk * blk, width), BF16)] * 2,
        in_specs=[SMEM, SMEM, VMEM, VMEM, pl.BlockSpec(memory_space=pl.ANY)],
        out_specs=[VMEM, VMEM],
        compiler_params=pltpu.CompilerParams(vmem_limit_bytes=20 * 1024 * 1024),
        cost_estimate=pl.CostEstimate(flops=10_000_000, bytes_accessed=6_291_456, transcendentals=0),
        name="densify",
    )(idx_up, idx_down, up, down, earlier)


def dot_nt(a, b):
    return lax.dot_general(a, b, (((1,), (1,)), ((), ())), preferred_element_type=F32)


def dot_nn(a, b):
    return lax.dot_general(a, b, (((1,), (0,)), ((), ())), preferred_element_type=F32)


def split3(value):
    high = value.astype(BF16).astype(F32)
    rest = value - high
    middle = rest.astype(BF16).astype(F32)
    return high, middle, rest - middle


def main_kernel(
    rows_ref, own_up, own_down, other_up, other_down, spent_ref, back_hbm, inverse_ref, give_ref, keep_ref, tiles_ref, weights, back_ref, in_sems, out_sems
):
    count = rows_ref.shape[0]
    tokens = (rows_ref.shape[1] - EXTRA) // 2
    width = count * LANES
    units = own_up.shape[0]
    per = units // LANES
    loads = [
        pltpu.make_async_copy(source, weights.at[n], in_sems.at[n])
        for n, source in enumerate((own_up, own_down, other_up, other_down))
    ]
    for load in loads:
        load.start()
    squares = jnp.zeros((tokens, LANES), F32)
    for j in range(count):
        x = rows_ref[j, :tokens, :].astype(F32)
        squares = squares + x * x
    mean_square = jnp.sum(squares, axis=-1, keepdims=True) / width
    inverse = 1.0 / jnp.sqrt(mean_square + eps)
    inverse_ref[...] = jnp.broadcast_to(inverse, inverse_ref.shape)
    for j in range(count):
        x = rows_ref[j, :tokens, :].astype(F32)
        gain = rows_ref[j, 2 * tokens :, :].astype(F32)[:1]
        tiles_ref[j] = (x * inverse * gain).astype(BF16)
    normed = jnp.concatenate([tiles_ref[j] for j in range(count)], axis=1)
    g_rows = jnp.concatenate([rows_ref[j, tokens : 2 * tokens, :] for j in range(count)], axis=1)
    stat = jnp.zeros((tokens, 1), F32)
    hiddens, g_pres = [], []
    for n, target in enumerate((keep_ref, give_ref)):
        loads[2 * n].wait()
        pre = dot_nt(normed, weights[2 * n])
        loads[2 * n + 1].wait()
        g_hidden = dot_nt(g_rows, weights[2 * n + 1])
        sig = 1.0 / (1.0 + jnp.exp(-pre))
        hidden = (pre * sig).astype(BF16)
        g_pre = (g_hidden * sig * (1.0 + pre * (1.0 - sig))).astype(BF16)
        stat = stat + jnp.sum(g_pre.astype(F32) * pre, axis=-1, keepdims=True)
        for k in range(per):
            at = slice(k * LANES, (k + 1) * LANES)
            target[k] = hidden[:, at]
            target[per + k] = g_pre[:, at]
        hiddens.append(hidden)
        g_pres.append(g_pre)
    stat_high, stat_low, _ = split3(stat)
    lane = lax.broadcasted_iota(jnp.int32, (tokens, LANES), 1)
    columns = jnp.zeros((tokens, LANES), F32)
    for k, part in enumerate((stat_high, stat_low) + split3(inverse)):
        columns = jnp.where(lane == k, part, columns)
    riding = jnp.transpose(columns)[:EXTRA].astype(BF16)
    step = 1024
    stores = []
    for n, s in enumerate(range(0, width, step)):
        back = dot_nn(g_pres[0], weights[0, :, s : s + step]) + dot_nn(
            g_pres[1], weights[2, :, s : s + step]
        )
        ffn = dot_nn(hiddens[0], weights[1, :, s : s + step]) + dot_nn(
            hiddens[1], weights[3, :, s : s + step]
        )
        for k in range(step // LANES):
            j = s // LANES + k
            at = slice(k * LANES, (k + 1) * LANES)
            back_ref[j, :tokens, :] = back[:, at].astype(BF16)
            back_ref[j, tokens : 2 * tokens, :] = ffn[:, at].astype(BF16)
            back_ref[j, 2 * tokens :, :] = riding
        at = pl.ds(s // LANES, step // LANES)
        stores.append(pltpu.make_async_copy(back_ref.at[at], back_hbm.at[at], out_sems.at[n]))
        stores[-1].start()
    for store in stores:
        store.wait()


def main(rows, own, other, spent):
    count = rows.shape[0]
    tokens = (rows.shape[1] - EXTRA) // 2
    units, width = own[0].shape
    per = units // LANES
    return pl.pallas_call(
        main_kernel,
        out_shape=(
            jax.ShapeDtypeStruct(spent.shape, BF16),
            jax.ShapeDtypeStruct((tokens, LANES), F32),
            jax.ShapeDtypeStruct((2 * per, tokens, LANES), BF16),
            jax.ShapeDtypeStruct((2 * per, tokens, LANES), BF16),
        ),
        in_specs=[VMEM] + [HBM] * 5,
        out_specs=[HBM, VMEM, VMEM, VMEM],
        scratch_shapes=[
            pltpu.VMEM((count, tokens, LANES), BF16),
            pltpu.VMEM((4, units, width), BF16),
            pltpu.VMEM(spent.shape, BF16),
            pltpu.SemaphoreType.DMA((4,)),
            pltpu.SemaphoreType.DMA((width // 1024,)),
        ],
        input_output_aliases={5: 0},
        compiler_params=pltpu.CompilerParams(vmem_limit_bytes=MAIN_VMEM * 1024 * 1024),
        cost_estimate=pl.CostEstimate(flops=2_200_000_000, bytes_accessed=16_000_000, transcendentals=65_536),
        name="forward_backward",
    )(rows, *own, *other, spent)


def normalize_kernel(rows_ref, inverse_ref, tiles_ref):
    count = rows_ref.shape[0]
    tokens = (rows_ref.shape[1] - EXTRA) // 2
    inverse = inverse_ref[...]
    for j in range(count):
        x = rows_ref[j, :tokens, :].astype(F32)
        gain = rows_ref[j, 2 * tokens :, :].astype(F32)[:1]
        tiles_ref[j] = (x * inverse * gain).astype(BF16)
        tiles_ref[count + j] = rows_ref[j, tokens : 2 * tokens, :]


def normalize(rows, inverse):
    count = rows.shape[0]
    tokens = (rows.shape[1] - EXTRA) // 2
    return pl.pallas_call(
        normalize_kernel,
        out_shape=jax.ShapeDtypeStruct((2 * count, tokens, LANES), BF16),
        in_specs=[VMEM, VMEM],
        out_specs=VMEM,
        compiler_params=pltpu.CompilerParams(vmem_limit_bytes=12 * 1024 * 1024),
        cost_estimate=pl.CostEstimate(flops=4_000_000, bytes_accessed=4_000_000, transcendentals=0),
        name="normalize",
    )(rows, inverse)


def grads_kernel(idx_up, idx_down, mine_ref, keep_ref, theirs_ref, given_ref, up_ref, down_ref, dense):
    hblk, blk, wide = up_ref.shape
    per = hblk * blk // LANES
    count = mine_ref.shape[0] // 2
    lower = lax.broadcasted_iota(jnp.int32, (1, LANES), 1) < blk
    group = 8

    def left(n):
        tiles = [
            jnp.concatenate([keep_ref[n * per + k], given_ref[n * per + k]], axis=0)
            for k in range(per)
        ]
        return jnp.concatenate(tiles, axis=1)

    for n, first, idx, out in ((0, count, idx_down, down_ref), (1, 0, idx_up, up_ref)):
        turned = jnp.transpose(left(n))
        for s in range(0, count, group):
            rows = jnp.concatenate(
                [
                    jnp.concatenate([mine_ref[first + j], theirs_ref[first + j]], axis=0)
                    for j in range(s, s + group)
                ],
                axis=1,
            )
            dense[:, s * LANES : (s + group) * LANES] = dot_nn(turned, rows).astype(BF16)
        def step(j, carry, idx=idx, out=out):
            merged = []
            for c in range(hblk):
                e0, e1 = idx[c, 2 * j], idx[c, 2 * j + 1]
                rows = pl.ds(c * blk, blk)
                merged.append(
                    merge_tiles(
                        dense[rows, tile_at(e0 // 2)],
                        dense[rows, tile_at(e1 // 2)],
                        e0 % 2,
                        1 - e1 % 2,
                        1,
                        1,
                        lower,
                    )
                )
            for c in range(hblk):
                out[c, :, tile_at(j)] = merged[c]
            return carry

        lax.fori_loop(0, wide // LANES, step, 0, unroll=2)


def grads(idx_up, idx_down, mine, keep, theirs, given, shape, width):
    hblk, blk, _ = shape
    return pl.pallas_call(
        grads_kernel,
        out_shape=(jax.ShapeDtypeStruct(shape, BF16), jax.ShapeDtypeStruct(shape, BF16)),
        in_specs=[SMEM, SMEM, VMEM, VMEM, VMEM, VMEM],
        out_specs=[VMEM, VMEM],
        scratch_shapes=[pltpu.VMEM((hblk * blk, width), BF16)],
        compiler_params=PARAMS,
        cost_estimate=pl.CostEstimate(flops=1_000_000, bytes_accessed=100_000, transcendentals=0),
        name="weight_gradients",
    )(idx_up, idx_down, mine, keep, theirs, given)


def finish_kernel(width, parts_hbm, base_ref, gain_ref, cot_ref, out_ref, gain_out_ref, parts, riding_ref, sems):
    count = parts_hbm.shape[0]
    tokens = (parts_hbm.shape[1] - EXTRA) // 2
    group = 8
    riding_load = pltpu.make_async_copy(
        parts_hbm.at[:, pl.ds(2 * tokens, EXTRA)], riding_ref, sems.at[count // group]
    )
    riding_load.start()
    loads = []
    for n in range(count // group):
        at = pl.ds(n * group, group)
        loads.append(
            pltpu.make_async_copy(parts_hbm.at[at, pl.ds(0, tokens)], parts.at[at], sems.at[n])
        )
        loads[-1].start()
    riding_load.wait()
    row = lax.broadcasted_iota(jnp.int32, (LANES, LANES), 0)
    stats, inverses = [], []
    for half in range(2):
        riding = jnp.zeros((EXTRA, LANES), F32)
        for j in range(half, count, 2):
            riding = riding + riding_ref[j].astype(F32)
        first = riding_ref[half].astype(F32)
        summed = (riding[0:1] + riding[1:2]) / width
        inverse = first[2:3] + first[3:4] + first[4:5]
        turned = jnp.transpose(jnp.where(row == 0, summed, jnp.where(row == 1, inverse, 0.0)))
        stats.append(turned[:, 0:1])
        inverses.append(turned[:, 1:2])
    totals = [jnp.zeros((tokens, LANES), F32) for _ in range(2)]
    for n, load in enumerate(loads):
        load.wait()
        for j in range(n * group, (n + 1) * group):
            totals[j % 2] = totals[j % 2] + parts[j].astype(F32)
    gain = gain_ref[...].astype(F32)
    total_gain = jnp.zeros((1, LANES), F32)
    for half in range(2):
        at = pl.ds(half * tokens, tokens)
        scaled = base_ref[at, :].astype(F32) * inverses[half]
        out_ref[at, :] = (
            (totals[half] * gain - scaled * stats[half]) * inverses[half] + cot_ref[at, :].astype(F32)
        ).astype(BF16)
        total_gain = total_gain + jnp.sum(totals[half] * scaled, axis=0, keepdims=True)
    gain_out_ref[...] = total_gain


def finish(parts, base, gain, cot, width):
    count, rows, _ = parts.shape
    return pl.pallas_call(
        functools.partial(finish_kernel, width),
        out_shape=(
            jax.ShapeDtypeStruct(base.shape, BF16),
            jax.ShapeDtypeStruct((1, LANES), F32),
        ),
        in_specs=[HBM, VMEM, VMEM, VMEM],
        out_specs=[VMEM] * 2,
        scratch_shapes=[
            pltpu.VMEM((count, (rows - EXTRA) // 2, LANES), BF16),
            pltpu.VMEM((count, EXTRA, LANES), BF16),
            pltpu.SemaphoreType.DMA((count // 8 + 1,)),
        ],
        compiler_params=PARAMS,
        cost_estimate=pl.CostEstimate(flops=2_000_000, bytes_accessed=1_500_000, transcendentals=0),
        name="input_gradient",
    )(parts, base, gain, cot)


def outputs_kernel(odd_ref, parts_ref, base_ref, part_ref, out_base_ref, out_part_ref):
    count = parts_ref.shape[0]
    tokens = (parts_ref.shape[1] - EXTRA) // 2
    odd = odd_ref[0].astype(F32)
    for half in range(2):
        total = jnp.zeros((tokens, LANES), F32)
        for j in range(half, count, 2):
            total = total + parts_ref[j, tokens : 2 * tokens, :].astype(F32)
        at = pl.ds(half * tokens, tokens)
        part = part_ref[at, :].astype(F32)
        out_base_ref[at, :] = (base_ref[at, :].astype(F32) + odd * (part + total)).astype(BF16)
        out_part_ref[at, :] = ((1.0 - odd) * total).astype(BF16)


def outputs(odd, parts, base, part):
    return pl.pallas_call(
        outputs_kernel,
        out_shape=(jax.ShapeDtypeStruct(base.shape, BF16), jax.ShapeDtypeStruct(base.shape, BF16)),
        in_specs=[SMEM, VMEM, VMEM, VMEM],
        out_specs=[VMEM] * 2,
        compiler_params=PARAMS,
        cost_estimate=pl.CostEstimate(flops=2_000_000, bytes_accessed=1_500_000, transcendentals=0),
        name="section_outputs",
    )(odd[None], parts, base, part)


def per_device(
    sent_base,
    sent_part,
    cot_base,
    cot_part,
    norm_gain,
    up_blocks,
    down_blocks,
    up_index,
    down_index,
):
    count = lax.axis_size("dp")
    tokens, lanes = sent_base.shape[1:]
    width = count * lanes
    odd = lax.axis_index("pipe") % 2

    arrived_base = passed_along(sent_base[0], "pipe", 1)
    packed = pack(odd, cot_base[0], cot_part[0], norm_gain, count)
    packed = pack_base(arrived_base, packed)
    rows = exchange(packed)
    own = densify(up_index[0], down_index[0], up_blocks[0], down_blocks[0], width, packed)
    other = [other_core(array) for array in own]
    g_part = jnp.where(odd == 1, cot_base[0], jnp.zeros_like(cot_base[0]))
    back_part = passed_along(after(g_part, packed), "pipe", -1)
    rows, back_part = lax.optimization_barrier((rows, back_part))

    parts, inverse, give, keep = main(rows, own, other, packed)
    tiles = normalize(rows, inverse)
    theirs = other_core(tiles)
    given = other_core(give)
    arrived_part = passed_along(after(sent_part[0], inverse), "pipe", 1)
    up_grad, down_grad = grads(
        up_index[0], down_index[0], tiles, keep, theirs, given, up_blocks.shape[1:], width
    )
    part_rows = exchange(parts)
    up_grad, down_grad, arrived_part, part_rows = lax.optimization_barrier(
        (up_grad, down_grad, arrived_part, part_rows)
    )
    base_gradient, gain_gradient = finish(part_rows, arrived_base, norm_gain, cot_base[0], width)
    back_base = passed_along(base_gradient, "pipe", -1)
    out_base, out_part = outputs(odd, part_rows, arrived_base, arrived_part)
    return (
        out_base[None],
        out_part[None],
        back_base[None],
        back_part[None],
        up_grad[None],
        down_grad[None],
        gain_gradient,
    )


def solution(mesh):
    in_specs = (
        P("pipe", None, "dp"),
        P("pipe", None, "dp"),
        P("pipe", None, "dp"),
        P("pipe", None, "dp"),
        P("pipe", "dp"),
        P("pipe", "dp", None, None),
        P("pipe", "dp", None, None),
        P("pipe", "dp", None),
        P("pipe", "dp", None),
    )
    out_specs = (
        P("pipe", None, "dp"),
        P("pipe", None, "dp"),
        P("pipe", None, "dp"),
        P("pipe", None, "dp"),
        P("pipe", "dp", None, None),
        P("pipe", "dp", None, None),
        P("pipe", "dp"),
    )
    return jax.shard_map(
        per_device, mesh=mesh, in_specs=in_specs, out_specs=out_specs, check_vma=False
    )
```

```python
import functools

import jax
import jax.numpy as jnp
from jax import lax
from jax.experimental import pallas as pl
from jax.experimental.pallas import tpu as pltpu
from jax.sharding import PartitionSpec as P

eps = 1e-05
LANES = 128
MAIN_VMEM = 24
EXTRA = 16
F32 = jnp.float32
BF16 = jnp.bfloat16
VMEM = pl.BlockSpec(memory_space=pltpu.VMEM)
SMEM = pl.BlockSpec(memory_space=pltpu.SMEM)
HBM = pl.BlockSpec(memory_space=pltpu.HBM)
PARAMS = pltpu.CompilerParams(vmem_limit_bytes=40 * 1024 * 1024)


def passed_along(shard, axis, by):
    count = lax.axis_size(axis)
    return lax.ppermute(shard, axis, [(i, (i + by) % count) for i in range(count)])


def other_core(shard):
    count = lax.axis_size("dp")
    return lax.ppermute(shard, "dp", [(i, i ^ 1) for i in range(count)])


def after(value, earlier):
    return lax.optimization_barrier((value, earlier))[0]


def exchange(chunks):
    return lax.all_to_all(chunks, "dp", 0, 0, tiled=True)


def pack_kernel(odd_ref, cot_base_hbm, cot_part_hbm, gain_hbm, out_ref, cot_base_ref, cot_part_ref, gain_ref, chunk, sems, in_sems):
    count = out_ref.shape[0]
    loads = [
        pltpu.make_async_copy(source, target, in_sems.at[n])
        for n, (source, target) in enumerate(
            ((cot_base_hbm, cot_base_ref), (cot_part_hbm, cot_part_ref), (gain_hbm, gain_ref))
        )
    ]
    for load in loads:
        load.start()
    for load in loads:
        load.wait()
    half = cot_base_ref.shape[0] // 2
    odd = odd_ref[0] == 1
    copies = []
    for n in range(2):
        at = pl.ds(n * half, half)
        chunk[n, :half, :] = jnp.where(odd, cot_base_ref[at, :], cot_part_ref[at, :])
        chunk[n, half:, :] = jnp.broadcast_to(gain_ref[...].astype(F32), (EXTRA, LANES)).astype(BF16)
    for j in range(count):
        copies.append(
            pltpu.make_async_copy(
                chunk.at[j % 2], out_ref.at[j, pl.ds(half, half + EXTRA)], sems.at[j]
            )
        )
        copies[-1].start()
    for copy in copies:
        copy.wait()


def pack(odd, cot_base, cot_part, gain, count):
    tokens = cot_base.shape[0]
    return pl.pallas_call(
        pack_kernel,
        out_shape=jax.ShapeDtypeStruct((count, tokens + EXTRA, LANES), BF16),
        in_specs=[SMEM, HBM, HBM, HBM],
        out_specs=HBM,
        scratch_shapes=[
            pltpu.VMEM(cot_base.shape, BF16),
            pltpu.VMEM(cot_part.shape, BF16),
            pltpu.VMEM(gain.shape, BF16),
            pltpu.VMEM((2, tokens // 2 + EXTRA, LANES), BF16),
            pltpu.SemaphoreType.DMA((count,)),
            pltpu.SemaphoreType.DMA((3,)),
        ],
        compiler_params=pltpu.CompilerParams(vmem_limit_bytes=60 * 1024 * 1024),
        cost_estimate=pl.CostEstimate(flops=1_000_000, bytes_accessed=1_500_000, transcendentals=0),
        name="pack_cotangent",
    )(odd[None], cot_base, cot_part, gain)


def pack_base_kernel(base_ref, packed_ref, out_ref, sems):
    count = out_ref.shape[0]
    half = base_ref.shape[0] // 2
    copies = []
    for j in range(count):
        copies.append(
            pltpu.make_async_copy(
                base_ref.at[pl.ds((j % 2) * half, half)], out_ref.at[j, pl.ds(0, half)], sems.at[j]
            )
        )
        copies[-1].start()
    for copy in copies:
        copy.wait()


def pack_base(base, packed):
    count = packed.shape[0]
    return pl.pallas_call(
        pack_base_kernel,
        out_shape=jax.ShapeDtypeStruct(packed.shape, BF16),
        in_specs=[VMEM, HBM],
        out_specs=HBM,
        scratch_shapes=[pltpu.SemaphoreType.DMA((count,))],
        input_output_aliases={1: 0},
        compiler_params=pltpu.CompilerParams(vmem_limit_bytes=16 * 1024 * 1024),
        cost_estimate=pl.CostEstimate(flops=1_000, bytes_accessed=1_000_000, transcendentals=0),
        name="pack_base",
    )(base, packed)


def merge_tiles(tile0, tile1, turned0, turned1, kept0, kept1, lower):
    low = jnp.where(lower, 1.0, 0.0).astype(BF16)
    high = jnp.where(lower, 0.0, 1.0).astype(BF16)
    swapped = tile1 * low + tile0 * high
    swapped = jnp.concatenate([swapped[:, 64:], swapped[:, :64]], axis=1)
    first = jnp.where(lower, kept0 * (1 - turned0), 0).astype(F32).astype(BF16)
    second = jnp.where(lower, 0, kept1 * (1 - turned1)).astype(F32).astype(BF16)
    third = jnp.where(lower, kept0 * turned0, kept1 * turned1).astype(F32).astype(BF16)
    return tile0 * first + tile1 * second + swapped * third


def tile_at(n):
    return pl.ds(pl.multiple_of(n * LANES, LANES), LANES)


def densify_kernel(idx_up, idx_down, up_ref, down_ref, after_ref, dense_up, dense_down):
    hblk, blk, wide = up_ref.shape
    kept = idx_up.shape[1]
    tiles = dense_up.shape[1] // LANES
    lower = lax.broadcasted_iota(jnp.int32, (1, LANES), 1) < blk
    for idx, src, dense in ((idx_up, up_ref, dense_up), (idx_down, down_ref, dense_down)):

        def step(j, ats, idx=idx, src=src, dense=dense):
            plans, next_ats = [], []
            for c in range(hblk):
                p0 = jnp.minimum(ats[c], kept - 1)
                m0 = jnp.where((ats[c] < kept) & (idx[c, p0] == 2 * j), 1, 0)
                middle = ats[c] + m0
                p1 = jnp.minimum(middle, kept - 1)
                m1 = jnp.where((middle < kept) & (idx[c, p1] == 2 * j + 1), 1, 0)
                plans.append((p0, m0, p1, m1))
                next_ats.append(middle + m1)
            loaded = [
                (src[c, :, tile_at(p0 // 2)], src[c, :, tile_at(p1 // 2)])
                for c, (p0, m0, p1, m1) in enumerate(plans)
            ]
            merged = [
                merge_tiles(tile0, tile1, p0 % 2, 1 - p1 % 2, m0, m1, lower)
                for (tile0, tile1), (p0, m0, p1, m1) in zip(loaded, plans)
            ]
            for c in range(hblk):
                dense[pl.ds(c * blk, blk), tile_at(j)] = merged[c]
            return tuple(next_ats)

        lax.fori_loop(0, tiles, step, (jnp.int32(0),) * hblk, unroll=2)


def densify(idx_up, idx_down, up, down, width, earlier):
    hblk, blk, _ = up.shape
    return pl.pallas_call(
        densify_kernel,
        out_shape=[jax.ShapeDtypeStruct((hblk * blk, width), BF16)] * 2,
        in_specs=[SMEM, SMEM, VMEM, VMEM, pl.BlockSpec(memory_space=pl.ANY)],
        out_specs=[VMEM, VMEM],
        compiler_params=pltpu.CompilerParams(vmem_limit_bytes=20 * 1024 * 1024),
        cost_estimate=pl.CostEstimate(flops=10_000_000, bytes_accessed=6_291_456, transcendentals=0),
        name="densify",
    )(idx_up, idx_down, up, down, earlier)


def dot_nt(a, b):
    return lax.dot_general(a, b, (((1,), (1,)), ((), ())), preferred_element_type=F32)


def dot_nn(a, b):
    return lax.dot_general(a, b, (((1,), (0,)), ((), ())), preferred_element_type=F32)


def split3(value):
    high = value.astype(BF16).astype(F32)
    rest = value - high
    middle = rest.astype(BF16).astype(F32)
    return high, middle, rest - middle


def main_kernel(
    rows_ref, own_up, own_down, other_up, other_down, spent_ref, back_hbm, inverse_ref, give_ref, keep_ref, tiles_ref, weights, back_ref, in_sems, out_sems
):
    count = rows_ref.shape[0]
    tokens = (rows_ref.shape[1] - EXTRA) // 2
    width = count * LANES
    units = own_up.shape[0]
    per = units // LANES
    loads = [
        pltpu.make_async_copy(source, weights.at[n], in_sems.at[n])
        for n, source in enumerate((own_up, own_down, other_up, other_down))
    ]
    for load in loads:
        load.start()
    squares = jnp.zeros((tokens, LANES), F32)
    for j in range(count):
        x = rows_ref[j, :tokens, :].astype(F32)
        squares = squares + x * x
    mean_square = jnp.sum(squares, axis=-1, keepdims=True) / width
    inverse = 1.0 / jnp.sqrt(mean_square + eps)
    inverse_ref[...] = jnp.broadcast_to(inverse, inverse_ref.shape)
    for j in range(count):
        x = rows_ref[j, :tokens, :].astype(F32)
        gain = rows_ref[j, 2 * tokens :, :].astype(F32)[:1]
        tiles_ref[j] = (x * inverse * gain).astype(BF16)
    normed = jnp.concatenate([tiles_ref[j] for j in range(count)], axis=1)
    g_rows = jnp.concatenate([rows_ref[j, tokens : 2 * tokens, :] for j in range(count)], axis=1)
    stat = jnp.zeros((tokens, 1), F32)
    hiddens, g_pres = [], []
    for n, target in enumerate((keep_ref, give_ref)):
        loads[2 * n].wait()
        pre = dot_nt(normed, weights[2 * n])
        loads[2 * n + 1].wait()
        g_hidden = dot_nt(g_rows, weights[2 * n + 1])
        sig = 1.0 / (1.0 + jnp.exp(-pre))
        hidden = (pre * sig).astype(BF16)
        g_pre = (g_hidden * sig * (1.0 + pre * (1.0 - sig))).astype(BF16)
        stat = stat + jnp.sum(g_pre.astype(F32) * pre, axis=-1, keepdims=True)
        for k in range(per):
            at = slice(k * LANES, (k + 1) * LANES)
            target[k] = hidden[:, at]
            target[per + k] = g_pre[:, at]
        hiddens.append(hidden)
        g_pres.append(g_pre)
    stat_high, stat_low, _ = split3(stat)
    lane = lax.broadcasted_iota(jnp.int32, (tokens, LANES), 1)
    columns = jnp.zeros((tokens, LANES), F32)
    for k, part in enumerate((stat_high, stat_low) + split3(inverse)):
        columns = jnp.where(lane == k, part, columns)
    riding = jnp.transpose(columns)[:EXTRA].astype(BF16)
    step = 1024
    stores = []
    for n, s in enumerate(range(0, width, step)):
        back = dot_nn(g_pres[0], weights[0, :, s : s + step]) + dot_nn(
            g_pres[1], weights[2, :, s : s + step]
        )
        ffn = dot_nn(hiddens[0], weights[1, :, s : s + step]) + dot_nn(
            hiddens[1], weights[3, :, s : s + step]
        )
        for k in range(step // LANES):
            j = s // LANES + k
            at = slice(k * LANES, (k + 1) * LANES)
            back_ref[j, :tokens, :] = back[:, at].astype(BF16)
            back_ref[j, tokens : 2 * tokens, :] = ffn[:, at].astype(BF16)
            back_ref[j, 2 * tokens :, :] = riding
        at = pl.ds(s // LANES, step // LANES)
        stores.append(pltpu.make_async_copy(back_ref.at[at], back_hbm.at[at], out_sems.at[n]))
        stores[-1].start()
    for store in stores:
        store.wait()


def main(rows, own, other, spent):
    count = rows.shape[0]
    tokens = (rows.shape[1] - EXTRA) // 2
    units, width = own[0].shape
    per = units // LANES
    return pl.pallas_call(
        main_kernel,
        out_shape=(
            jax.ShapeDtypeStruct(spent.shape, BF16),
            jax.ShapeDtypeStruct((tokens, LANES), F32),
            jax.ShapeDtypeStruct((2 * per, tokens, LANES), BF16),
            jax.ShapeDtypeStruct((2 * per, tokens, LANES), BF16),
        ),
        in_specs=[VMEM] + [HBM] * 5,
        out_specs=[HBM, VMEM, VMEM, VMEM],
        scratch_shapes=[
            pltpu.VMEM((count, tokens, LANES), BF16),
            pltpu.VMEM((4, units, width), BF16),
            pltpu.VMEM(spent.shape, BF16),
            pltpu.SemaphoreType.DMA((4,)),
            pltpu.SemaphoreType.DMA((width // 1024,)),
        ],
        input_output_aliases={5: 0},
        compiler_params=pltpu.CompilerParams(vmem_limit_bytes=MAIN_VMEM * 1024 * 1024),
        cost_estimate=pl.CostEstimate(flops=2_200_000_000, bytes_accessed=16_000_000, transcendentals=65_536),
        name="forward_backward",
    )(rows, *own, *other, spent)


def normalize_kernel(rows_ref, inverse_ref, tiles_ref):
    count = rows_ref.shape[0]
    tokens = (rows_ref.shape[1] - EXTRA) // 2
    inverse = inverse_ref[...]
    for j in range(count):
        x = rows_ref[j, :tokens, :].astype(F32)
        gain = rows_ref[j, 2 * tokens :, :].astype(F32)[:1]
        tiles_ref[j] = (x * inverse * gain).astype(BF16)
        tiles_ref[count + j] = rows_ref[j, tokens : 2 * tokens, :]


def normalize(rows, inverse):
    count = rows.shape[0]
    tokens = (rows.shape[1] - EXTRA) // 2
    return pl.pallas_call(
        normalize_kernel,
        out_shape=jax.ShapeDtypeStruct((2 * count, tokens, LANES), BF16),
        in_specs=[VMEM, VMEM],
        out_specs=VMEM,
        compiler_params=pltpu.CompilerParams(vmem_limit_bytes=12 * 1024 * 1024),
        cost_estimate=pl.CostEstimate(flops=4_000_000, bytes_accessed=4_000_000, transcendentals=0),
        name="normalize",
    )(rows, inverse)


def grads_kernel(idx_up, idx_down, mine_ref, keep_ref, theirs_ref, given_ref, up_ref, down_ref, dense):
    hblk, blk, wide = up_ref.shape
    per = hblk * blk // LANES
    count = mine_ref.shape[0] // 2
    lower = lax.broadcasted_iota(jnp.int32, (1, LANES), 1) < blk
    group = 8

    def left(n):
        tiles = [
            jnp.concatenate([keep_ref[n * per + k], given_ref[n * per + k]], axis=0)
            for k in range(per)
        ]
        return jnp.concatenate(tiles, axis=1)

    for n, first, idx, out in ((0, count, idx_down, down_ref), (1, 0, idx_up, up_ref)):
        turned = jnp.transpose(left(n))
        for s in range(0, count, group):
            rows = jnp.concatenate(
                [
                    jnp.concatenate([mine_ref[first + j], theirs_ref[first + j]], axis=0)
                    for j in range(s, s + group)
                ],
                axis=1,
            )
            dense[:, s * LANES : (s + group) * LANES] = dot_nn(turned, rows).astype(BF16)
        def step(j, carry, idx=idx, out=out):
            merged = []
            for c in range(hblk):
                e0, e1 = idx[c, 2 * j], idx[c, 2 * j + 1]
                rows = pl.ds(c * blk, blk)
                merged.append(
                    merge_tiles(
                        dense[rows, tile_at(e0 // 2)],
                        dense[rows, tile_at(e1 // 2)],
                        e0 % 2,
                        1 - e1 % 2,
                        1,
                        1,
                        lower,
                    )
                )
            for c in range(hblk):
                out[c, :, tile_at(j)] = merged[c]
            return carry

        lax.fori_loop(0, wide // LANES, step, 0, unroll=2)


def grads(idx_up, idx_down, mine, keep, theirs, given, shape, width):
    hblk, blk, _ = shape
    return pl.pallas_call(
        grads_kernel,
        out_shape=(jax.ShapeDtypeStruct(shape, BF16), jax.ShapeDtypeStruct(shape, BF16)),
        in_specs=[SMEM, SMEM, VMEM, VMEM, VMEM, VMEM],
        out_specs=[VMEM, VMEM],
        scratch_shapes=[pltpu.VMEM((hblk * blk, width), BF16)],
        compiler_params=PARAMS,
        cost_estimate=pl.CostEstimate(flops=1_000_000, bytes_accessed=100_000, transcendentals=0),
        name="weight_gradients",
    )(idx_up, idx_down, mine, keep, theirs, given)


def finish_kernel(width, parts_hbm, base_ref, gain_ref, cot_ref, out_ref, gain_out_ref, parts, riding_ref, sems):
    count = parts_hbm.shape[0]
    tokens = (parts_hbm.shape[1] - EXTRA) // 2
    group = 8
    riding_load = pltpu.make_async_copy(
        parts_hbm.at[:, pl.ds(2 * tokens, EXTRA)], riding_ref, sems.at[count // group]
    )
    riding_load.start()
    loads = []
    for n in range(count // group):
        at = pl.ds(n * group, group)
        loads.append(
            pltpu.make_async_copy(parts_hbm.at[at, pl.ds(0, tokens)], parts.at[at], sems.at[n])
        )
        loads[-1].start()
    riding_load.wait()
    row = lax.broadcasted_iota(jnp.int32, (LANES, LANES), 0)
    stats, inverses = [], []
    for half in range(2):
        riding = jnp.zeros((EXTRA, LANES), F32)
        for j in range(half, count, 2):
            riding = riding + riding_ref[j].astype(F32)
        first = riding_ref[half].astype(F32)
        summed = (riding[0:1] + riding[1:2]) / width
        inverse = first[2:3] + first[3:4] + first[4:5]
        turned = jnp.transpose(jnp.where(row == 0, summed, jnp.where(row == 1, inverse, 0.0)))
        stats.append(turned[:, 0:1])
        inverses.append(turned[:, 1:2])
    totals = [jnp.zeros((tokens, LANES), F32) for _ in range(2)]
    for n, load in enumerate(loads):
        load.wait()
        for j in range(n * group, (n + 1) * group):
            totals[j % 2] = totals[j % 2] + parts[j].astype(F32)
    gain = gain_ref[...].astype(F32)
    total_gain = jnp.zeros((1, LANES), F32)
    for half in range(2):
        at = pl.ds(half * tokens, tokens)
        scaled = base_ref[at, :].astype(F32) * inverses[half]
        out_ref[at, :] = (
            (totals[half] * gain - scaled * stats[half]) * inverses[half] + cot_ref[at, :].astype(F32)
        ).astype(BF16)
        total_gain = total_gain + jnp.sum(totals[half] * scaled, axis=0, keepdims=True)
    gain_out_ref[...] = total_gain


def finish(parts, base, gain, cot, width):
    count, rows, _ = parts.shape
    return pl.pallas_call(
        functools.partial(finish_kernel, width),
        out_shape=(
            jax.ShapeDtypeStruct(base.shape, BF16),
            jax.ShapeDtypeStruct((1, LANES), F32),
        ),
        in_specs=[HBM, VMEM, VMEM, VMEM],
        out_specs=[VMEM] * 2,
        scratch_shapes=[
            pltpu.VMEM((count, (rows - EXTRA) // 2, LANES), BF16),
            pltpu.VMEM((count, EXTRA, LANES), BF16),
            pltpu.SemaphoreType.DMA((count // 8 + 1,)),
        ],
        compiler_params=PARAMS,
        cost_estimate=pl.CostEstimate(flops=2_000_000, bytes_accessed=1_500_000, transcendentals=0),
        name="input_gradient",
    )(parts, base, gain, cot)


def outputs_kernel(
    odd_ref, parts_hbm, base_ref, part_ref, back_part_ref, out_base_ref, out_part_ref, back_part_out, parts, sems
):
    count = parts_hbm.shape[0]
    tokens = (parts_hbm.shape[1] - EXTRA) // 2
    group = 8
    loads = []
    for n in range(count // group):
        at = pl.ds(n * group, group)
        loads.append(
            pltpu.make_async_copy(parts_hbm.at[at, pl.ds(tokens, tokens)], parts.at[at], sems.at[n])
        )
        loads[-1].start()
    odd = odd_ref[0].astype(F32)
    back_part_out[...] = back_part_ref[...]
    totals = [jnp.zeros((tokens, LANES), F32) for _ in range(2)]
    for n, load in enumerate(loads):
        load.wait()
        for j in range(n * group, (n + 1) * group):
            totals[j % 2] = totals[j % 2] + parts[j].astype(F32)
    for half in range(2):
        at = pl.ds(half * tokens, tokens)
        part = part_ref[at, :].astype(F32)
        out_base_ref[at, :] = (base_ref[at, :].astype(F32) + odd * (part + totals[half])).astype(BF16)
        out_part_ref[at, :] = ((1.0 - odd) * totals[half]).astype(BF16)


def outputs(odd, parts, base, part, back_part):
    count, rows, _ = parts.shape
    return pl.pallas_call(
        outputs_kernel,
        out_shape=[jax.ShapeDtypeStruct(base.shape, BF16)] * 3,
        in_specs=[SMEM, HBM, VMEM, VMEM, VMEM],
        out_specs=[VMEM] * 3,
        scratch_shapes=[
            pltpu.VMEM((count, (rows - EXTRA) // 2, LANES), BF16),
            pltpu.SemaphoreType.DMA((count // 8,)),
        ],
        compiler_params=PARAMS,
        cost_estimate=pl.CostEstimate(flops=2_000_000, bytes_accessed=1_500_000, transcendentals=0),
        name="section_outputs",
    )(odd[None], parts, base, part, back_part)


def per_device(
    sent_base,
    sent_part,
    cot_base,
    cot_part,
    norm_gain,
    up_blocks,
    down_blocks,
    up_index,
    down_index,
):
    count = lax.axis_size("dp")
    tokens, lanes = sent_base.shape[1:]
    width = count * lanes
    odd = lax.axis_index("pipe") % 2

    arrived_base = passed_along(sent_base[0], "pipe", 1)
    packed = pack(odd, cot_base[0], cot_part[0], norm_gain, count)
    packed = pack_base(arrived_base, packed)
    rows = exchange(packed)
    own = densify(up_index[0], down_index[0], up_blocks[0], down_blocks[0], width, packed)
    other = [other_core(array) for array in own]
    g_part = jnp.where(odd == 1, cot_base[0], jnp.zeros_like(cot_base[0]))
    back_part = passed_along(after(g_part, packed), "pipe", -1)
    rows, back_part = lax.optimization_barrier((rows, back_part))

    parts, inverse, give, keep = main(rows, own, other, packed)
    tiles = normalize(rows, inverse)
    theirs = other_core(tiles)
    given = other_core(give)
    arrived_part = passed_along(after(sent_part[0], inverse), "pipe", 1)
    up_grad, down_grad = grads(
        up_index[0], down_index[0], tiles, keep, theirs, given, up_blocks.shape[1:], width
    )
    part_rows = exchange(parts)
    up_grad, down_grad, arrived_part, part_rows = lax.optimization_barrier(
        (up_grad, down_grad, arrived_part, part_rows)
    )
    base_gradient, gain_gradient = finish(part_rows, arrived_base, norm_gain, cot_base[0], width)
    back_base = passed_along(base_gradient[None], "pipe", -1)
    out_base, out_part, back_part = outputs(
        odd, part_rows, arrived_base, arrived_part, back_part
    )
    return (
        out_base[None],
        out_part[None],
        back_base,
        back_part[None],
        up_grad[None],
        down_grad[None],
        gain_gradient,
    )


def solution(mesh):
    in_specs = (
        P("pipe", None, "dp"),
        P("pipe", None, "dp"),
        P("pipe", None, "dp"),
        P("pipe", None, "dp"),
        P("pipe", "dp"),
        P("pipe", "dp", None, None),
        P("pipe", "dp", None, None),
        P("pipe", "dp", None),
        P("pipe", "dp", None),
    )
    out_specs = (
        P("pipe", None, "dp"),
        P("pipe", None, "dp"),
        P("pipe", None, "dp"),
        P("pipe", None, "dp"),
        P("pipe", "dp", None, None),
        P("pipe", "dp", None, None),
        P("pipe", "dp"),
    )
    return jax.shard_map(
        per_device, mesh=mesh, in_specs=in_specs, out_specs=out_specs, check_vma=False
    )
```

```python
import functools

import jax
import jax.numpy as jnp
from jax import lax
from jax.experimental import pallas as pl
from jax.experimental.pallas import tpu as pltpu
from jax.sharding import PartitionSpec as P

eps = 1e-05
LANES = 128
MAIN_VMEM = 24
EXTRA = 16
F32 = jnp.float32
BF16 = jnp.bfloat16
VMEM = pl.BlockSpec(memory_space=pltpu.VMEM)
SMEM = pl.BlockSpec(memory_space=pltpu.SMEM)
HBM = pl.BlockSpec(memory_space=pltpu.HBM)
PARAMS = pltpu.CompilerParams(vmem_limit_bytes=40 * 1024 * 1024)


def passed_along(shard, axis, by):
    count = lax.axis_size(axis)
    return lax.ppermute(shard, axis, [(i, (i + by) % count) for i in range(count)])


def other_core(shard):
    count = lax.axis_size("dp")
    return lax.ppermute(shard, "dp", [(i, i ^ 1) for i in range(count)])


def after(value, earlier):
    return lax.optimization_barrier((value, earlier))[0]


def exchange(chunks):
    return lax.all_to_all(chunks, "dp", 0, 0, tiled=True)


def pack_kernel(odd_ref, cot_base_hbm, cot_part_hbm, gain_hbm, out_ref, cot_base_ref, cot_part_ref, gain_ref, chunk, sems, in_sems):
    count = out_ref.shape[0]
    loads = [
        pltpu.make_async_copy(source, target, in_sems.at[n])
        for n, (source, target) in enumerate(
            ((cot_base_hbm, cot_base_ref), (cot_part_hbm, cot_part_ref), (gain_hbm, gain_ref))
        )
    ]
    for load in loads:
        load.start()
    for load in loads:
        load.wait()
    half = cot_base_ref.shape[0] // 2
    odd = odd_ref[0] == 1
    copies = []
    for n in range(2):
        at = pl.ds(n * half, half)
        chunk[n, :half, :] = jnp.where(odd, cot_base_ref[at, :], cot_part_ref[at, :])
        chunk[n, half:, :] = jnp.broadcast_to(gain_ref[...].astype(F32), (EXTRA, LANES)).astype(BF16)
    for j in range(count // 2):
        copies.append(
            pltpu.make_async_copy(
                chunk, out_ref.at[pl.ds(2 * j, 2), pl.ds(half, half + EXTRA)], sems.at[j]
            )
        )
        copies[-1].start()
    for copy in copies:
        copy.wait()


def pack(odd, cot_base, cot_part, gain, count):
    tokens = cot_base.shape[0]
    return pl.pallas_call(
        pack_kernel,
        out_shape=jax.ShapeDtypeStruct((count, tokens + EXTRA, LANES), BF16),
        in_specs=[SMEM, HBM, HBM, HBM],
        out_specs=HBM,
        scratch_shapes=[
            pltpu.VMEM(cot_base.shape, BF16),
            pltpu.VMEM(cot_part.shape, BF16),
            pltpu.VMEM(gain.shape, BF16),
            pltpu.VMEM((2, tokens // 2 + EXTRA, LANES), BF16),
            pltpu.SemaphoreType.DMA((count,)),
            pltpu.SemaphoreType.DMA((3,)),
        ],
        compiler_params=pltpu.CompilerParams(vmem_limit_bytes=60 * 1024 * 1024),
        cost_estimate=pl.CostEstimate(flops=1_000_000, bytes_accessed=1_500_000, transcendentals=0),
        name="pack_cotangent",
    )(odd[None], cot_base, cot_part, gain)


def pack_base_kernel(base_ref, packed_ref, out_ref, sems):
    count = out_ref.shape[0]
    halves, half, _ = base_ref.shape
    copies = []
    for j in range(count // halves):
        copies.append(
            pltpu.make_async_copy(
                base_ref, out_ref.at[pl.ds(j * halves, halves), pl.ds(0, half)], sems.at[j]
            )
        )
        copies[-1].start()
    for copy in copies:
        copy.wait()


def pack_base(base, packed):
    count = packed.shape[0]
    return pl.pallas_call(
        pack_base_kernel,
        out_shape=jax.ShapeDtypeStruct(packed.shape, BF16),
        in_specs=[VMEM, HBM],
        out_specs=HBM,
        scratch_shapes=[pltpu.SemaphoreType.DMA((count,))],
        input_output_aliases={1: 0},
        compiler_params=pltpu.CompilerParams(vmem_limit_bytes=16 * 1024 * 1024),
        cost_estimate=pl.CostEstimate(flops=1_000, bytes_accessed=1_000_000, transcendentals=0),
        name="pack_base",
    )(base.reshape(2, -1, LANES), packed)


def merge_tiles(tile0, tile1, turned0, turned1, kept0, kept1, lower):
    low = jnp.where(lower, 1.0, 0.0).astype(BF16)
    high = jnp.where(lower, 0.0, 1.0).astype(BF16)
    swapped = tile1 * low + tile0 * high
    swapped = jnp.concatenate([swapped[:, 64:], swapped[:, :64]], axis=1)
    first = jnp.where(lower, kept0 * (1 - turned0), 0).astype(F32).astype(BF16)
    second = jnp.where(lower, 0, kept1 * (1 - turned1)).astype(F32).astype(BF16)
    third = jnp.where(lower, kept0 * turned0, kept1 * turned1).astype(F32).astype(BF16)
    return tile0 * first + tile1 * second + swapped * third


def tile_at(n):
    return pl.ds(pl.multiple_of(n * LANES, LANES), LANES)


def densify_kernel(idx_up, idx_down, up_ref, down_ref, after_ref, dense_up, dense_down):
    hblk, blk, wide = up_ref.shape
    kept = idx_up.shape[1]
    tiles = dense_up.shape[1] // LANES
    lower = lax.broadcasted_iota(jnp.int32, (1, LANES), 1) < blk
    for idx, src, dense in ((idx_up, up_ref, dense_up), (idx_down, down_ref, dense_down)):

        def step(j, ats, idx=idx, src=src, dense=dense):
            plans, next_ats = [], []
            for c in range(hblk):
                p0 = jnp.minimum(ats[c], kept - 1)
                m0 = jnp.where((ats[c] < kept) & (idx[c, p0] == 2 * j), 1, 0)
                middle = ats[c] + m0
                p1 = jnp.minimum(middle, kept - 1)
                m1 = jnp.where((middle < kept) & (idx[c, p1] == 2 * j + 1), 1, 0)
                plans.append((p0, m0, p1, m1))
                next_ats.append(middle + m1)
            loaded = [
                (src[c, :, tile_at(p0 // 2)], src[c, :, tile_at(p1 // 2)])
                for c, (p0, m0, p1, m1) in enumerate(plans)
            ]
            merged = [
                merge_tiles(tile0, tile1, p0 % 2, 1 - p1 % 2, m0, m1, lower)
                for (tile0, tile1), (p0, m0, p1, m1) in zip(loaded, plans)
            ]
            for c in range(hblk):
                dense[pl.ds(c * blk, blk), tile_at(j)] = merged[c]
            return tuple(next_ats)

        lax.fori_loop(0, tiles, step, (jnp.int32(0),) * hblk, unroll=2)


def densify(idx_up, idx_down, up, down, width, earlier):
    hblk, blk, _ = up.shape
    return pl.pallas_call(
        densify_kernel,
        out_shape=[jax.ShapeDtypeStruct((hblk * blk, width), BF16)] * 2,
        in_specs=[SMEM, SMEM, VMEM, VMEM, pl.BlockSpec(memory_space=pl.ANY)],
        out_specs=[VMEM, VMEM],
        compiler_params=pltpu.CompilerParams(vmem_limit_bytes=20 * 1024 * 1024),
        cost_estimate=pl.CostEstimate(flops=10_000_000, bytes_accessed=6_291_456, transcendentals=0),
        name="densify",
    )(idx_up, idx_down, up, down, earlier)


def dot_nt(a, b):
    return lax.dot_general(a, b, (((1,), (1,)), ((), ())), preferred_element_type=F32)


def dot_nn(a, b):
    return lax.dot_general(a, b, (((1,), (0,)), ((), ())), preferred_element_type=F32)


def split3(value):
    high = value.astype(BF16).astype(F32)
    rest = value - high
    middle = rest.astype(BF16).astype(F32)
    return high, middle, rest - middle


def main_kernel(
    rows_ref, own_up, own_down, other_up, other_down, spent_ref, back_hbm, inverse_ref, give_ref, keep_ref, tiles_ref, weights, back_ref, in_sems, out_sems
):
    count = rows_ref.shape[0]
    tokens = (rows_ref.shape[1] - EXTRA) // 2
    width = count * LANES
    units = own_up.shape[0]
    per = units // LANES
    loads = [
        pltpu.make_async_copy(source, weights.at[n], in_sems.at[n])
        for n, source in enumerate((own_up, own_down, other_up, other_down))
    ]
    for load in loads:
        load.start()
    squares = jnp.zeros((tokens, LANES), F32)
    for j in range(count):
        x = rows_ref[j, :tokens, :].astype(F32)
        squares = squares + x * x
    mean_square = jnp.sum(squares, axis=-1, keepdims=True) / width
    inverse = 1.0 / jnp.sqrt(mean_square + eps)
    inverse_ref[...] = jnp.broadcast_to(inverse, inverse_ref.shape)
    for j in range(count):
        x = rows_ref[j, :tokens, :].astype(F32)
        gain = rows_ref[j, 2 * tokens :, :].astype(F32)[:1]
        tiles_ref[j] = (x * inverse * gain).astype(BF16)
    normed = jnp.concatenate([tiles_ref[j] for j in range(count)], axis=1)
    g_rows = jnp.concatenate([rows_ref[j, tokens : 2 * tokens, :] for j in range(count)], axis=1)
    stat = jnp.zeros((tokens, 1), F32)
    hiddens, g_pres = [], []
    for n, target in enumerate((keep_ref, give_ref)):
        loads[2 * n].wait()
        pre = dot_nt(normed, weights[2 * n])
        loads[2 * n + 1].wait()
        g_hidden = dot_nt(g_rows, weights[2 * n + 1])
        sig = 1.0 / (1.0 + jnp.exp(-pre))
        hidden = (pre * sig).astype(BF16)
        g_pre = (g_hidden * sig * (1.0 + pre * (1.0 - sig))).astype(BF16)
        stat = stat + jnp.sum(g_pre.astype(F32) * pre, axis=-1, keepdims=True)
        for k in range(per):
            at = slice(k * LANES, (k + 1) * LANES)
            target[k] = hidden[:, at]
            target[per + k] = g_pre[:, at]
        hiddens.append(hidden)
        g_pres.append(g_pre)
    stat_high, stat_low, _ = split3(stat)
    lane = lax.broadcasted_iota(jnp.int32, (tokens, LANES), 1)
    columns = jnp.zeros((tokens, LANES), F32)
    for k, part in enumerate((stat_high, stat_low) + split3(inverse)):
        columns = jnp.where(lane == k, part, columns)
    riding = jnp.transpose(columns)[:EXTRA].astype(BF16)
    step = 1024
    stores = []
    for n, s in enumerate(range(0, width, step)):
        back = dot_nn(g_pres[0], weights[0, :, s : s + step]) + dot_nn(
            g_pres[1], weights[2, :, s : s + step]
        )
        ffn = dot_nn(hiddens[0], weights[1, :, s : s + step]) + dot_nn(
            hiddens[1], weights[3, :, s : s + step]
        )
        for k in range(step // LANES):
            j = s // LANES + k
            at = slice(k * LANES, (k + 1) * LANES)
            back_ref[j, :tokens, :] = back[:, at].astype(BF16)
            back_ref[j, tokens : tokens + EXTRA, :] = riding
            back_ref[j, tokens + EXTRA :, :] = ffn[:, at].astype(BF16)
        at = pl.ds(s // LANES, step // LANES)
        stores.append(pltpu.make_async_copy(back_ref.at[at], back_hbm.at[at], out_sems.at[n]))
        stores[-1].start()
    for store in stores:
        store.wait()


def main(rows, own, other, spent):
    count = rows.shape[0]
    tokens = (rows.shape[1] - EXTRA) // 2
    units, width = own[0].shape
    per = units // LANES
    return pl.pallas_call(
        main_kernel,
        out_shape=(
            jax.ShapeDtypeStruct(spent.shape, BF16),
            jax.ShapeDtypeStruct((tokens, LANES), F32),
            jax.ShapeDtypeStruct((2 * per, tokens, LANES), BF16),
            jax.ShapeDtypeStruct((2 * per, tokens, LANES), BF16),
        ),
        in_specs=[VMEM] + [HBM] * 5,
        out_specs=[HBM, VMEM, VMEM, VMEM],
        scratch_shapes=[
            pltpu.VMEM((count, tokens, LANES), BF16),
            pltpu.VMEM((4, units, width), BF16),
            pltpu.VMEM(spent.shape, BF16),
            pltpu.SemaphoreType.DMA((4,)),
            pltpu.SemaphoreType.DMA((width // 1024,)),
        ],
        input_output_aliases={5: 0},
        compiler_params=pltpu.CompilerParams(vmem_limit_bytes=MAIN_VMEM * 1024 * 1024),
        cost_estimate=pl.CostEstimate(flops=2_200_000_000, bytes_accessed=16_000_000, transcendentals=65_536),
        name="forward_backward",
    )(rows, *own, *other, spent)


def normalize_kernel(rows_ref, inverse_ref, tiles_ref):
    count = rows_ref.shape[0]
    tokens = (rows_ref.shape[1] - EXTRA) // 2
    inverse = inverse_ref[...]
    for j in range(count):
        x = rows_ref[j, :tokens, :].astype(F32)
        gain = rows_ref[j, 2 * tokens :, :].astype(F32)[:1]
        tiles_ref[j] = (x * inverse * gain).astype(BF16)
        tiles_ref[count + j] = rows_ref[j, tokens : 2 * tokens, :]


def normalize(rows, inverse):
    count = rows.shape[0]
    tokens = (rows.shape[1] - EXTRA) // 2
    return pl.pallas_call(
        normalize_kernel,
        out_shape=jax.ShapeDtypeStruct((2 * count, tokens, LANES), BF16),
        in_specs=[VMEM, VMEM],
        out_specs=VMEM,
        compiler_params=pltpu.CompilerParams(vmem_limit_bytes=12 * 1024 * 1024),
        cost_estimate=pl.CostEstimate(flops=4_000_000, bytes_accessed=4_000_000, transcendentals=0),
        name="normalize",
    )(rows, inverse)


def grads_kernel(idx_up, idx_down, mine_ref, keep_ref, theirs_ref, given_ref, up_ref, down_ref, dense):
    hblk, blk, wide = up_ref.shape
    per = hblk * blk // LANES
    count = mine_ref.shape[0] // 2
    lower = lax.broadcasted_iota(jnp.int32, (1, LANES), 1) < blk
    group = 8

    def left(n):
        tiles = [
            jnp.concatenate([keep_ref[n * per + k], given_ref[n * per + k]], axis=0)
            for k in range(per)
        ]
        return jnp.concatenate(tiles, axis=1)

    for n, first, idx, out in ((0, count, idx_down, down_ref), (1, 0, idx_up, up_ref)):
        turned = jnp.transpose(left(n))
        for s in range(0, count, group):
            rows = jnp.concatenate(
                [
                    jnp.concatenate([mine_ref[first + j], theirs_ref[first + j]], axis=0)
                    for j in range(s, s + group)
                ],
                axis=1,
            )
            dense[:, s * LANES : (s + group) * LANES] = dot_nn(turned, rows).astype(BF16)
        def step(j, carry, idx=idx, out=out):
            merged = []
            for c in range(hblk):
                e0, e1 = idx[c, 2 * j], idx[c, 2 * j + 1]
                rows = pl.ds(c * blk, blk)
                merged.append(
                    merge_tiles(
                        dense[rows, tile_at(e0 // 2)],
                        dense[rows, tile_at(e1 // 2)],
                        e0 % 2,
                        1 - e1 % 2,
                        1,
                        1,
                        lower,
                    )
                )
            for c in range(hblk):
                out[c, :, tile_at(j)] = merged[c]
            return carry

        lax.fori_loop(0, wide // LANES, step, 0, unroll=2)


def grads(idx_up, idx_down, mine, keep, theirs, given, shape, width):
    hblk, blk, _ = shape
    return pl.pallas_call(
        grads_kernel,
        out_shape=(jax.ShapeDtypeStruct(shape, BF16), jax.ShapeDtypeStruct(shape, BF16)),
        in_specs=[SMEM, SMEM, VMEM, VMEM, VMEM, VMEM],
        out_specs=[VMEM, VMEM],
        scratch_shapes=[pltpu.VMEM((hblk * blk, width), BF16)],
        compiler_params=PARAMS,
        cost_estimate=pl.CostEstimate(flops=1_000_000, bytes_accessed=100_000, transcendentals=0),
        name="weight_gradients",
    )(idx_up, idx_down, mine, keep, theirs, given)


def finish_kernel(width, parts_hbm, base_ref, gain_ref, cot_ref, out_ref, gain_out_ref, parts, sems):
    count = parts_hbm.shape[0]
    tokens = (parts_hbm.shape[1] - EXTRA) // 2
    group = 8
    loads = []
    for n in range(count // group):
        at = pl.ds(n * group, group)
        loads.append(
            pltpu.make_async_copy(parts_hbm.at[at, pl.ds(0, tokens + EXTRA)], parts.at[at], sems.at[n])
        )
        loads[-1].start()
    totals = [jnp.zeros((tokens, LANES), F32) for _ in range(2)]
    for n, load in enumerate(loads):
        load.wait()
        for j in range(n * group, (n + 1) * group):
            totals[j % 2] = totals[j % 2] + parts[j, :tokens, :].astype(F32)
    row = lax.broadcasted_iota(jnp.int32, (LANES, LANES), 0)
    stats, inverses = [], []
    for half in range(2):
        riding = jnp.zeros((EXTRA, LANES), F32)
        for j in range(half, count, 2):
            riding = riding + parts[j, tokens:, :].astype(F32)
        first = parts[half, tokens:, :].astype(F32)
        summed = (riding[0:1] + riding[1:2]) / width
        inverse = first[2:3] + first[3:4] + first[4:5]
        turned = jnp.transpose(jnp.where(row == 0, summed, jnp.where(row == 1, inverse, 0.0)))
        stats.append(turned[:, 0:1])
        inverses.append(turned[:, 1:2])
    gain = gain_ref[...].astype(F32)
    total_gain = jnp.zeros((1, LANES), F32)
    for half in range(2):
        at = pl.ds(half * tokens, tokens)
        scaled = base_ref[at, :].astype(F32) * inverses[half]
        out_ref[at, :] = (
            (totals[half] * gain - scaled * stats[half]) * inverses[half] + cot_ref[at, :].astype(F32)
        ).astype(BF16)
        total_gain = total_gain + jnp.sum(totals[half] * scaled, axis=0, keepdims=True)
    gain_out_ref[...] = total_gain


def finish(parts, base, gain, cot, width):
    count, rows, _ = parts.shape
    return pl.pallas_call(
        functools.partial(finish_kernel, width),
        out_shape=(
            jax.ShapeDtypeStruct(base.shape, BF16),
            jax.ShapeDtypeStruct((1, LANES), F32),
        ),
        in_specs=[HBM, VMEM, VMEM, VMEM],
        out_specs=[VMEM] * 2,
        scratch_shapes=[
            pltpu.VMEM((count, (rows + EXTRA) // 2, LANES), BF16),
            pltpu.SemaphoreType.DMA((count // 8,)),
        ],
        compiler_params=PARAMS,
        cost_estimate=pl.CostEstimate(flops=2_000_000, bytes_accessed=1_500_000, transcendentals=0),
        name="input_gradient",
    )(parts, base, gain, cot)


def outputs_kernel(
    odd_ref, parts_hbm, base_ref, part_ref, back_part_ref, out_base_ref, out_part_ref, back_part_out, parts, sems
):
    count = parts_hbm.shape[0]
    tokens = (parts_hbm.shape[1] - EXTRA) // 2
    group = 8
    loads = []
    for n in range(count // group):
        at = pl.ds(n * group, group)
        loads.append(
            pltpu.make_async_copy(parts_hbm.at[at, pl.ds(tokens + EXTRA, tokens)], parts.at[at], sems.at[n])
        )
        loads[-1].start()
    odd = odd_ref[0].astype(F32)
    back_part_out[...] = back_part_ref[...]
    totals = [jnp.zeros((tokens, LANES), F32) for _ in range(2)]
    for n, load in enumerate(loads):
        load.wait()
        for j in range(n * group, (n + 1) * group):
            totals[j % 2] = totals[j % 2] + parts[j].astype(F32)
    for half in range(2):
        at = pl.ds(half * tokens, tokens)
        part = part_ref[at, :].astype(F32)
        out_base_ref[at, :] = (base_ref[at, :].astype(F32) + odd * (part + totals[half])).astype(BF16)
        out_part_ref[at, :] = ((1.0 - odd) * totals[half]).astype(BF16)


def outputs(odd, parts, base, part, back_part):
    count, rows, _ = parts.shape
    return pl.pallas_call(
        outputs_kernel,
        out_shape=[jax.ShapeDtypeStruct(base.shape, BF16)] * 3,
        in_specs=[SMEM, HBM, VMEM, VMEM, VMEM],
        out_specs=[VMEM] * 3,
        scratch_shapes=[
            pltpu.VMEM((count, (rows - EXTRA) // 2, LANES), BF16),
            pltpu.SemaphoreType.DMA((count // 8,)),
        ],
        compiler_params=PARAMS,
        cost_estimate=pl.CostEstimate(flops=2_000_000, bytes_accessed=1_500_000, transcendentals=0),
        name="section_outputs",
    )(odd[None], parts, base, part, back_part)


def per_device(
    sent_base,
    sent_part,
    cot_base,
    cot_part,
    norm_gain,
    up_blocks,
    down_blocks,
    up_index,
    down_index,
):
    count = lax.axis_size("dp")
    tokens, lanes = sent_base.shape[1:]
    width = count * lanes
    odd = lax.axis_index("pipe") % 2

    arrived_base = passed_along(sent_base[0], "pipe", 1)
    packed = pack(odd, cot_base[0], cot_part[0], norm_gain, count)
    packed = pack_base(arrived_base, packed)
    rows = exchange(packed)
    own = densify(up_index[0], down_index[0], up_blocks[0], down_blocks[0], width, packed)
    other = [other_core(array) for array in own]
    g_part = jnp.where(odd == 1, cot_base[0], jnp.zeros_like(cot_base[0]))
    back_part = passed_along(after(g_part, packed), "pipe", -1)
    rows, back_part = lax.optimization_barrier((rows, back_part))

    parts, inverse, give, keep = main(rows, own, other, packed)
    tiles = normalize(rows, inverse)
    theirs = other_core(tiles)
    given = other_core(give)
    arrived_part = passed_along(after(sent_part[0], inverse), "pipe", 1)
    up_grad, down_grad = grads(
        up_index[0], down_index[0], tiles, keep, theirs, given, up_blocks.shape[1:], width
    )
    part_rows = exchange(parts)
    up_grad, down_grad, arrived_part, part_rows = lax.optimization_barrier(
        (up_grad, down_grad, arrived_part, part_rows)
    )
    base_gradient, gain_gradient = finish(part_rows, arrived_base, norm_gain, cot_base[0], width)
    back_base = passed_along(base_gradient[None], "pipe", -1)
    out_base, out_part, back_part = outputs(
        odd, part_rows, arrived_base, arrived_part, back_part
    )
    return (
        out_base[None],
        out_part[None],
        back_base,
        back_part[None],
        up_grad[None],
        down_grad[None],
        gain_gradient,
    )


def solution(mesh):
    in_specs = (
        P("pipe", None, "dp"),
        P("pipe", None, "dp"),
        P("pipe", None, "dp"),
        P("pipe", None, "dp"),
        P("pipe", "dp"),
        P("pipe", "dp", None, None),
        P("pipe", "dp", None, None),
        P("pipe", "dp", None),
        P("pipe", "dp", None),
    )
    out_specs = (
        P("pipe", None, "dp"),
        P("pipe", None, "dp"),
        P("pipe", None, "dp"),
        P("pipe", None, "dp"),
        P("pipe", "dp", None, None),
        P("pipe", "dp", None, None),
        P("pipe", "dp"),
    )
    return jax.shard_map(
        per_device, mesh=mesh, in_specs=in_specs, out_specs=out_specs, check_vma=False
    )
```
